512 devices in a mesh: dp: 64 (over z, y), mp: 8 (over x, core).
Axes of the slice: x: 4, y: 4, z: 16, core: 2. Of those that a mesh axis runs over, the one named last changes fastest.
Arguments:
- hidden_rows: bfloat16 [64, 384, 4096], P('dp'), may hold values from -6 to 6
- norm_gain: float32 [4096], replicated, may hold values from 0.5 to 1.5
- w_query: bfloat16 [4096, 2048], P('dp', 'mp'), may hold values from -0.01171875 to 0.01171875
- w_key: bfloat16 [4096, 2048], P('dp', 'mp'), may hold values from -0.09375 to 0.09375
- w_value: bfloat16 [4096, 2048], P('dp', 'mp'), may hold values from -0.09375 to 0.09375
- head_cotangent: bfloat16 [64, 484, 2048], P('dp', None, 'mp'), may hold values from -6 to 6
- prompt_cotangent: bfloat16 [64, 100, 4096], P('dp'), may hold values from -0.29882812 to 0.29882812
- prompt_master: float32 [100, 4096], P(None, 'dp'), may hold values from -5 to 5
- prompt_first: float32 [100, 4096], P(None, 'dp'), may hold values from -0.6 to 0.6
- prompt_second: float32 [100, 4096], P(None, 'dp'), may hold values from 0.01 to 1
- row_factor: float32 [4096, 100], P('dp'), may hold values from 0.5 to 1.5
- row_first: float32 [4096, 100], P('dp'), may hold values from -3 to 3
- row_second: float32 [4096, 100], P('dp'), may hold values from 0.1 to 10
- col_factor: float32 [4096, 4096], P('dp', 'mp'), may hold values from 0.5 to 1.5
- col_first: float32 [4096, 4096], P('dp', 'mp'), may hold values from -0.6 to 0.6
- col_second: float32 [4096, 4096], P('dp', 'mp'), may hold values from 0.01 to 1
- row_tenant: int32 [64], P('dp'), may hold values from 0 to 4095
- tenant_slot: int32 [4096], replicated, may hold values from 0 to 4095, each once
Outputs:
- prompt_out: float32 [100, 4096], P(None, 'dp')
- prompt_first_out: float32 [100, 4096], P(None, 'dp')
- prompt_second_out: float32 [100, 4096], P(None, 'dp')
- row_out: float32 [4096, 100], P('dp')
- row_first_out: float32 [4096, 100], P('dp')
- row_second_out: float32 [4096, 100], P('dp')
- col_out: float32 [4096, 4096], P('dp', 'mp')
- col_first_out: float32 [4096, 4096], P('dp', 'mp')
- col_second_out: float32 [4096, 4096], P('dp', 'mp')
The draws below stay inside these ranges and needn't reach their ends.
Inputs may be any that keep to these rules, and one draw needn't show every extreme that they name: `row_tenant`: each row's tenant. `tenant_slot`: each tenant has one slot, each slot one tenant; slot s is held by dp index s // 64.
All inputs are finite; a program needn't handle non-finite values.
Results may differ from the reference program's by a relative error of at most 0.0073.
Values may be sent and summed in bfloat16 or wider, within the bound.
No kernel may reach another device: no remote copies, remote signals or barrier semaphores. Data moves between devices by JAX's collectives and lax.ppermute only.
A program may use at most 64 MiB of HBM per device.

```python
import math
import jax
import jax.numpy as jnp
import numpy as np
from jax import lax

D = 4096
HEAD_DIM = 64
PROMPT = 100
SEQ = 384
TENANTS = 4096
ROWS = 64
LENGTH = 484
INNER = 2048


def with_ends(drawn, stream_key, low, top_value):
    spot = [jax.random.randint(jax.random.fold_in(stream_key, axis), (), 0, length) for axis, length in enumerate(drawn.shape)]
    widest = drawn.shape.index(max(drawn.shape))
    neighbour = spot[:widest] + [(spot[widest] + 1) % drawn.shape[widest]] + spot[widest + 1:]
    return drawn.at[tuple(spot)].set(low).at[tuple(neighbour)].set(top_value)


def block_scale(own_key, dims, pieces, smallest, high):
    loudness = 1.0
    for position, blocks in pieces:
        steps = jax.random.uniform(jax.random.fold_in(jax.random.fold_in(own_key, 6), position), (blocks,), jnp.float32, smallest / len(pieces), high / len(pieces))
        loudness = loudness * jnp.repeat(jnp.exp(steps), dims[position] // blocks).reshape((-1,) + (1,) * (len(dims) - 1 - position))
    return loudness


def cumulative_ranks(number_of, lean):
    portions = [(1 << 20) // math.isqrt(standing ** lean) + 1 for standing in range(1, number_of + 1)]
    width = 1 + sum(portions) // (1 << 30)
    return np.cumsum(np.array([max(1, weight // width) for weight in portions]))


def ranked_ids(rng, dims, number_of, skew):
    listing = cumulative_ranks(number_of, skew)
    pick = jax.random.randint(jax.random.fold_in(rng, 1), dims, 0, int(listing[number_of - 1]))
    grade = jnp.searchsorted(jnp.asarray(listing, jnp.int32), pick, side="right")
    return jax.random.permutation(jax.random.fold_in(rng, 2), number_of)[grade].astype(jnp.int32)


def noise(stream_key, extent, spread, reach, split=(), kind=jnp.bfloat16):
    values = spread * jax.random.normal(stream_key, extent, jnp.float32)
    if split:
        values = values * block_scale(stream_key, extent, split, -0.22, 0.18)
    return jnp.clip(values, -reach, reach).astype(kind)


def setup_inputs(seed: int = 0) -> dict:
    splits = jax.random.split(jax.random.key(seed), 19)
    hidden_rows = noise(splits[0], (ROWS, SEQ, D), 1.0, 6.0, ((0, 64),))
    norm_gain = jnp.clip(1.0 + 0.1 * jax.random.normal(splits[1], (D,), jnp.float32), 0.5, 1.5)
    w_query = noise(splits[2], (D, INNER), (D * HEAD_DIM) ** -0.5, 0.01171875, ((0, 64), (1, 8)))
    w_key = noise(splits[3], (D, INNER), D ** -0.5, 0.09375, ((0, 64), (1, 8)))
    w_value = noise(splits[4], (D, INNER), D ** -0.5, 0.09375, ((0, 64), (1, 8)))
    head_cotangent = noise(splits[5], (ROWS, LENGTH, INNER), 1.0, 6.0, ((0, 64), (2, 8)))
    prompt_cotangent = noise(splits[6], (ROWS, PROMPT, D), 0.05, 0.29882812, ((0, 64),))
    prompt_master = noise(splits[7], (PROMPT, D), 1.0, 5.0, ((1, 64),), jnp.float32)
    prompt_first = noise(splits[8], (PROMPT, D), 0.1, 0.6, ((1, 64),), jnp.float32)
    prompt_second = jnp.clip(jnp.exp(math.log(1.0) - 4.6051702 * jax.random.uniform(splits[9], (PROMPT, D), jnp.float32) ** block_scale(splits[9], (PROMPT, D), ((1, 64),), -0.2, 0.2)), 0.01, 1.0)
    row_factor = jnp.clip(0.5 + 1.0 * jax.random.uniform(splits[10], (TENANTS, PROMPT), jnp.float32) ** block_scale(splits[10], (TENANTS, PROMPT), ((0, 64),), -0.2, 0.2), 0.5, 1.5)
    row_first = noise(splits[11], (TENANTS, PROMPT), 0.5, 3.0, ((0, 64),), jnp.float32)
    row_second = jnp.clip(jnp.exp(math.log(10.0) - 4.6051702 * jax.random.uniform(splits[12], (TENANTS, PROMPT), jnp.float32) ** block_scale(splits[12], (TENANTS, PROMPT), ((0, 64),), -0.2, 0.2)), 0.1, 10.0)
    col_factor = jnp.clip(0.5 + 1.0 * jax.random.uniform(splits[13], (TENANTS, D), jnp.float32) ** block_scale(splits[13], (TENANTS, D), ((0, 64), (1, 8)), -0.2, 0.2), 0.5, 1.5)
    col_first = noise(splits[14], (TENANTS, D), 0.1, 0.6, ((0, 64), (1, 8)), jnp.float32)
    col_second = jnp.clip(jnp.exp(math.log(1.0) - 4.6051702 * jax.random.uniform(splits[15], (TENANTS, D), jnp.float32) ** block_scale(splits[15], (TENANTS, D), ((0, 64), (1, 8)), -0.2, 0.2)), 0.01, 1.0)
    row_tenant = with_ends(ranked_ids(splits[16], (ROWS,), TENANTS, 2), jax.random.fold_in(splits[16], 3), 0, TENANTS - 1).astype(jnp.int32)
    tenant_slot = jax.random.permutation(splits[17], TENANTS).astype(jnp.int32)
    return {"hidden_rows": hidden_rows, "norm_gain": norm_gain, "w_query": w_query, "w_key": w_key, "w_value": w_value, "head_cotangent": head_cotangent, "prompt_cotangent": prompt_cotangent, "prompt_master": prompt_master, "prompt_first": prompt_first, "prompt_second": prompt_second, "row_factor": row_factor, "row_first": row_first, "row_second": row_second, "col_factor": col_factor, "col_first": col_first, "col_second": col_second, "row_tenant": row_tenant, "tenant_slot": tenant_slot}


beta_first = 0.9
beta_second = 0.99
learn_rate = 0.01
adam_epsilon = 1e-08
norm_epsilon = 1e-06

def adam_step(param, moment_one, moment_two, gradient):
    first_new = beta_first * moment_one + (1.0 - beta_first) * gradient
    second_new = beta_second * moment_two + (1.0 - beta_second) * gradient * gradient
    return (param - learn_rate * first_new / (jnp.sqrt(second_new) + adam_epsilon), first_new, second_new)

def rounded(values):
    return lax.optimization_barrier(values.astype(jnp.bfloat16)).astype(jnp.float32)

def row_gradient(tokens_row, resid_grad, heads_grad, prompt_base, factor_rows, factor_cols, norm_gain, w_query, w_key, w_value):
    base_float = prompt_base.astype(jnp.float32)
    prompt_act = (base_float * factor_rows[:, None] * factor_cols[None, :]).astype(jnp.bfloat16)
    stacked = jnp.concatenate([prompt_act, tokens_row], axis=0)
    floated = stacked.astype(jnp.float32)
    inverse = lax.rsqrt(lax.optimization_barrier(jnp.mean(floated * floated, axis=-1, keepdims=True)) + norm_epsilon)
    unit_rows = floated * inverse
    normed = (unit_rows * norm_gain[None, :]).astype(jnp.bfloat16)
    length = stacked.shape[0]
    heads = w_query.shape[1] // HEAD_DIM
    queries = rounded(jnp.dot(normed, w_query, preferred_element_type=jnp.float32)).reshape(length, heads, HEAD_DIM)
    keyset = rounded(jnp.dot(normed, w_key, preferred_element_type=jnp.float32)).reshape(length, heads, HEAD_DIM)
    valueset = rounded(jnp.dot(normed, w_value, preferred_element_type=jnp.float32)).reshape(length, heads, HEAD_DIM)
    upstream = heads_grad.astype(jnp.float32).reshape(length, heads, HEAD_DIM)
    scores = jnp.einsum('qhd,khd->hqk', queries, keyset)
    exponent = jnp.exp(scores)
    attend = exponent / lax.optimization_barrier(jnp.sum(exponent, axis=-1, keepdims=True))
    attend_low = rounded(attend)
    grad_prob = jnp.einsum('qhd,khd->hqk', upstream, valueset)
    row_dot = lax.optimization_barrier(jnp.sum(attend * grad_prob, axis=-1, keepdims=True))
    grad_score = rounded(attend * (grad_prob - row_dot))
    grad_query = jnp.einsum('hqk,khd->qhd', grad_score[:, :PROMPT, :], keyset).astype(jnp.bfloat16)
    grad_key = jnp.einsum('hqk,qhd->khd', grad_score[:, :, :PROMPT], queries).astype(jnp.bfloat16)
    grad_value = jnp.einsum('hqk,qhd->khd', attend_low[:, :, :PROMPT], upstream).astype(jnp.bfloat16)
    contract = (((1,), (1,)), ((), ()))
    head_total = lax.dot_general(grad_query.reshape(PROMPT, -1), w_query, contract, preferred_element_type=jnp.float32)
    head_total = head_total + lax.dot_general(grad_key.reshape(PROMPT, -1), w_key, contract, preferred_element_type=jnp.float32)
    head_total = head_total + lax.dot_general(grad_value.reshape(PROMPT, -1), w_value, contract, preferred_element_type=jnp.float32)
    scaled = head_total * norm_gain[None, :]
    unit_prompt = unit_rows[:PROMPT]
    grad_norm = inverse[:PROMPT] * (scaled - unit_prompt * lax.optimization_barrier(jnp.mean(scaled * unit_prompt, axis=-1, keepdims=True)))
    grad_prompt = resid_grad.astype(jnp.float32) + grad_norm
    grad_rows = lax.optimization_barrier(jnp.sum(grad_prompt * base_float * factor_cols[None, :], axis=-1))
    grad_cols = lax.optimization_barrier(jnp.sum(grad_prompt * base_float * factor_rows[:, None], axis=0))
    grad_base = grad_prompt * factor_rows[:, None] * factor_cols[None, :]
    return (grad_rows, grad_cols, grad_base)

def reference(hidden_rows, norm_gain, w_query, w_key, w_value, head_cotangent, prompt_cotangent, prompt_master, prompt_first, prompt_second, row_factor, row_first, row_second, col_factor, col_first, col_second, row_tenant, tenant_slot):
    slot_ids = tenant_slot[row_tenant].astype(jnp.int32)
    its_rows = row_factor[slot_ids]
    its_cols = col_factor[slot_ids]
    prompt_base = prompt_master.astype(jnp.bfloat16)

    def one_row(packed):
        tokens_row, resid_grad, heads_grad, factor_rows, factor_cols = packed
        return row_gradient(tokens_row, resid_grad, heads_grad, prompt_base, factor_rows, factor_cols, norm_gain, w_query, w_key, w_value)
    grad_rows, grad_cols, grad_base = lax.map(one_row, (hidden_rows, prompt_cotangent, head_cotangent, its_rows, its_cols))
    prompt_grad = lax.optimization_barrier(jnp.sum(grad_base, axis=0))
    row_grad = jax.ops.segment_sum(grad_rows, slot_ids, num_segments=TENANTS)
    col_grad = jax.ops.segment_sum(grad_cols, slot_ids, num_segments=TENANTS)
    prompt_out, prompt_first_out, prompt_second_out = adam_step(prompt_master, prompt_first, prompt_second, prompt_grad)
    row_out, row_first_out, row_second_out = adam_step(row_factor, row_first, row_second, row_grad)
    col_out, col_first_out, col_second_out = adam_step(col_factor, col_first, col_second, col_grad)
    return (prompt_out, prompt_first_out, prompt_second_out, row_out, row_first_out, row_second_out, col_out, col_first_out, col_second_out)
```

```python
import jax
import jax.numpy as jnp
from jax import lax
from jax.experimental import pallas as pl
from jax.experimental.pallas import tpu as pltpu
from jax.sharding import Mesh, PartitionSpec as P

HEAD_DIM = 64
PROMPT = 100
PAD = 128
BLOCK = 16
LANES = 128

beta_first = 0.9
beta_second = 0.99
learn_rate = 0.01
adam_epsilon = 1e-08
norm_epsilon = 1e-06

ROWS_AXES = ("z", "y")
HEADS_AXES = ("x", "c")
BF16 = jnp.bfloat16
F32 = jnp.float32
VMEM_LIMIT = 48 * 1024 * 1024


def adam_step(param, moment_one, moment_two, gradient):
    first_new = beta_first * moment_one + (1.0 - beta_first) * gradient
    second_new = beta_second * moment_two + (1.0 - beta_second) * gradient * gradient
    return (
        param - learn_rate * first_new / (jnp.sqrt(second_new) + adam_epsilon),
        first_new,
        second_new,
    )


def dot(a, b, da, db):
    return lax.dot_general(a, b, (((da,), (db,)), ((), ())), preferred_element_type=F32)


def attention_kernel(qkv_ref, up_ref, grads_ref, along_ref):
    length = up_ref.shape[0]
    inner = up_ref.shape[1]
    column = lax.broadcasted_iota(jnp.int32, (length, length), 1)
    real_key = (column < PROMPT) | (column >= PAD)
    along = jnp.zeros((PAD, 1), F32)
    for head in range(inner // HEAD_DIM):
        at = head * HEAD_DIM
        query = qkv_ref[:, at : at + HEAD_DIM]
        key = qkv_ref[:, inner + at : inner + at + HEAD_DIM]
        value = qkv_ref[:, 2 * inner + at : 2 * inner + at + HEAD_DIM]
        up = up_ref[:, at : at + HEAD_DIM]
        exponent = jnp.where(real_key, jnp.exp(dot(query, key, 1, 1)), 0.0)
        attend = exponent / jnp.sum(exponent, axis=1, keepdims=True)
        grad_prob = dot(up, value, 1, 1)
        row_dot = jnp.sum(attend * grad_prob, axis=1, keepdims=True)
        grad_score = (attend * (grad_prob - row_dot)).astype(BF16)
        grad_query = dot(grad_score[:PAD, :], key, 1, 0).astype(BF16)
        grad_key = dot(grad_score[:, :PAD], query, 0, 0).astype(BF16)
        grad_value = dot(attend[:, :PAD].astype(BF16), up, 0, 0).astype(BF16)
        for place, (grad, low) in enumerate(
            ((grad_query, query), (grad_key, key), (grad_value, value))
        ):
            grads_ref[:, place * inner + at : place * inner + at + HEAD_DIM] = grad
            along = along + jnp.sum(
                grad.astype(F32) * low[:PAD].astype(F32), axis=1, keepdims=True
            )
    along_ref[...] = jnp.broadcast_to(along, along_ref.shape)


def attention(qkv, up):
    return pl.pallas_call(
        attention_kernel,
        out_shape=(
            jax.ShapeDtypeStruct((PAD, qkv.shape[1]), BF16),
            jax.ShapeDtypeStruct((PAD, LANES), F32),
        ),
        in_specs=[pl.BlockSpec(memory_space=pltpu.VMEM)] * 2,
        out_specs=(pl.BlockSpec(memory_space=pltpu.VMEM),) * 2,
        compiler_params=pltpu.CompilerParams(vmem_limit_bytes=VMEM_LIMIT),
    )(qkv, up)


def head_kernel(
    width, grads_ref, weight_ref, along_ref, act_ref, base_ref, cot_ref, gain_ref, scale_ref, out_ref
):
    step = pl.program_id(0)
    part = dot(grads_ref[...], weight_ref[...], 1, 1)
    inverse = scale_ref[:, 0:1]
    rows = scale_ref[:, 1:2]
    mine = scale_ref[:, 2:3]
    mean = along_ref[:, 0:1] * (1.0 / width)
    unit = act_ref[...].astype(F32) * inverse
    grad = inverse * (part * gain_ref[...] - unit * mean) + mine * cot_ref[...].astype(F32)
    cols = jnp.sum(grad * base_ref[...].astype(F32) * rows, axis=0, keepdims=True)
    size = part.shape[1]
    out_ref[:, pl.ds(pl.multiple_of(step * size, size), size)] = part.astype(BF16)
    high = cols.astype(BF16).astype(F32)
    low = cols - high
    pieces = [high[:, at : at + LANES] for at in range(0, size, LANES)]
    pieces += [low[:, at : at + LANES] for at in range(0, size, LANES)]
    spare = BLOCK - len(pieces)
    if spare:
        pieces.append(jnp.zeros((spare, LANES), F32))
    out_ref[pl.ds(pl.multiple_of(step * BLOCK, BLOCK), BLOCK), width:] = jnp.concatenate(
        pieces, axis=0
    ).astype(BF16)


def head_parts(grads, weights, along, act, base, cot, gain, scale, groups):
    width = act.shape[1]
    size = width // groups
    full = lambda shape: pl.BlockSpec(shape, lambda i: (0,) * len(shape))
    stripe = lambda rows: pl.BlockSpec((rows, size), lambda i: (0, i))
    return pl.pallas_call(
        lambda *refs: head_kernel(width, *refs),
        grid=(groups,),
        out_shape=jax.ShapeDtypeStruct((PAD, width + LANES), BF16),
        in_specs=[
            full(grads.shape),
            pl.BlockSpec((size, weights.shape[1]), lambda i: (i, 0)),
            full(along.shape),
            stripe(PAD),
            stripe(PAD),
            stripe(PAD),
            stripe(1),
            full(scale.shape),
        ],
        out_specs=full((PAD, width + LANES)),
        compiler_params=pltpu.CompilerParams(vmem_limit_bytes=VMEM_LIMIT),
    )(grads, weights, along, act, base, cot, gain, scale)


def prompt_kernel(pieces, got_ref, act_ref, base_ref, cot_ref, gain_ref, cols_ref, scale_ref, out_ref):
    width = act_ref.shape[1]
    total = got_ref[0, :, :].astype(F32)
    for source in range(1, got_ref.shape[0]):
        total = total + got_ref[source, :, :].astype(F32)
    inverse = scale_ref[:, 0:1]
    rows = scale_ref[:, 1:2]
    unit = act_ref[...].astype(F32) * inverse
    scaled = total[:, :width] * gain_ref[...]
    mean = jnp.sum(scaled * unit, axis=1, keepdims=True) * (1.0 / width)
    grad = cot_ref[...].astype(F32) + inverse * (scaled - unit * mean)
    times_cols = grad * cols_ref[...]
    grad_rows = jnp.sum(times_cols * base_ref[...].astype(F32), axis=1, keepdims=True)
    grad_base = times_cols * rows
    extra = total[:, width:]
    cols = extra[:pieces, :] + extra[pieces : 2 * pieces, :]
    half = LANES // 2
    swapped = jnp.concatenate([cols[:, half:], cols[:, :half]], axis=1)
    spare = BLOCK - 2 * pieces
    lane = lax.broadcasted_iota(jnp.int32, (spare, LANES), 1)
    index = lax.broadcasted_iota(jnp.int32, (BLOCK, LANES), 0)
    line = jnp.sum(
        jnp.where(
            lax.broadcasted_iota(jnp.int32, (BLOCK, LANES), 1) == index + half, grad_rows, 0.0
        ),
        axis=0,
        keepdims=True,
    )
    under = jnp.where(lax.broadcasted_iota(jnp.int32, (spare, LANES), 0) == 0, line, 0.0)
    tail = jnp.concatenate([cols, swapped, under], axis=0)
    first_half = lax.broadcasted_iota(jnp.int32, (BLOCK, LANES), 1) < half
    for pair in range(width // LANES):
        block = grad_base[:, pair * LANES : (pair + 1) * LANES]
        other = jnp.concatenate([block[:, half:], block[:, :half]], axis=1)
        out_ref[2 * pair, :, :] = jnp.where(first_half, block, tail).astype(BF16)
        out_ref[2 * pair + 1, :, :] = jnp.where(first_half, other, tail).astype(BF16)


def prompt_grads(got, act, base, cot, gain, cols, scale, group_size, pieces):
    return pl.pallas_call(
        lambda *refs: prompt_kernel(pieces, *refs),
        out_shape=jax.ShapeDtypeStruct((group_size, BLOCK, LANES), BF16),
        in_specs=[pl.BlockSpec(memory_space=pltpu.VMEM)] * 7,
        out_specs=pl.BlockSpec(memory_space=pltpu.VMEM),
        compiler_params=pltpu.CompilerParams(vmem_limit_bytes=VMEM_LIMIT),
    )(got, act, base, cot, gain, cols, scale)


def local(
    hidden_rows,
    norm_gain,
    w_query,
    w_key,
    w_value,
    head_cotangent,
    prompt_cotangent,
    prompt_master,
    prompt_first,
    prompt_second,
    row_factor,
    row_first,
    row_second,
    col_factor,
    col_first,
    col_second,
    row_tenant,
    tenant_slot,
):
    dp, mp = ROWS_AXES, HEADS_AXES
    group_size = lax.axis_size(dp)
    groups = lax.axis_size(mp)
    device = lax.axis_index(dp)
    member = lax.axis_index(mp)
    owned_count = row_factor.shape[0]
    col_width = col_factor.shape[1]
    width = hidden_rows.shape[2]
    own_cols = prompt_master.shape[1]
    half = LANES // 2
    pieces = col_width // LANES

    weights = jnp.concatenate([w_query, w_key, w_value], axis=1)
    weights_y = lax.all_gather(weights, "y", axis=0, tiled=True)

    slot = lax.dynamic_index_in_dim(tenant_slot, row_tenant[0], 0, keepdims=False)
    base_own = jnp.pad(prompt_master.astype(BF16), ((0, PAD - PROMPT), (0, 0)))
    base_block = lax.dynamic_slice_in_dim(base_own, member * BLOCK, BLOCK, 0)
    marks = jnp.stack([slot // owned_count, slot % owned_count]).astype(BF16)
    marks = jnp.pad(jnp.broadcast_to(marks[None, :], (BLOCK, 2)), ((0, 0), (0, half - 2)))
    sent = jnp.concatenate([base_block, marks], axis=1)
    sent, weights_y = lax.optimization_barrier((sent, weights_y))
    weights_all = lax.all_gather(weights_y, "z", axis=0, tiled=True)
    got = lax.all_to_all(
        jnp.broadcast_to(sent[None], (group_size, BLOCK, LANES)), dp, 0, 0, tiled=False
    )
    base_mine = jnp.transpose(got[:, :, :own_cols], (1, 0, 2)).reshape(BLOCK, width)
    base = lax.all_to_all(
        jnp.broadcast_to(base_mine[None], (groups, BLOCK, width)), mp, 0, 0, tiled=False
    ).reshape(PAD, width)
    owner_all = got[:, 0, half].astype(jnp.int32)
    place_all = got[:, 0, half + 1].astype(jnp.int32)
    picker = (
        (owner_all == device)[:, None]
        & (place_all[:, None] == lax.broadcasted_iota(jnp.int32, (group_size, owned_count), 1))
    ).astype(F32)

    row_term = jnp.dot(picker, row_factor, precision=lax.Precision.HIGHEST)
    col_term = jnp.dot(picker, col_factor, precision=lax.Precision.HIGHEST)
    terms = jnp.concatenate(
        [
            col_term.reshape(group_size, pieces, LANES),
            jnp.pad(row_term, ((0, 0), (0, LANES - PROMPT)))[:, None, :],
            jnp.zeros((group_size, 8 - pieces - 1, LANES), F32),
        ],
        axis=1,
    )
    terms = jnp.sum(lax.all_to_all(terms, dp, 0, 0, tiled=False), axis=0)
    factor_rows = terms[pieces]
    my_cols = terms[:pieces].reshape(col_width)
    factor_cols = lax.all_gather(my_cols, mp, axis=0, tiled=True)

    gain = norm_gain[None, :]
    hidden = hidden_rows[0].astype(F32)
    hidden_inverse = lax.rsqrt(jnp.mean(hidden * hidden, axis=-1, keepdims=True) + norm_epsilon)
    hidden_normed = (hidden * hidden_inverse * gain).astype(BF16)
    act = (base.astype(F32) * factor_rows[:, None] * factor_cols[None, :]).astype(BF16)
    act_float = act.astype(F32)
    inverse = lax.rsqrt(jnp.mean(act_float * act_float, axis=-1, keepdims=True) + norm_epsilon)
    prompt_normed = (act_float * inverse * gain).astype(BF16)
    normed = jnp.concatenate([prompt_normed, hidden_normed], axis=0)
    qkv = jnp.dot(normed, weights_all, preferred_element_type=F32).astype(BF16)
    upstream = jnp.concatenate(
        [
            jnp.pad(head_cotangent[0, :PROMPT], ((0, PAD - PROMPT), (0, 0))),
            head_cotangent[0, PROMPT:],
        ],
        axis=0,
    )
    grads, along = attention(qkv, upstream)

    cot = jnp.pad(prompt_cotangent[0], ((0, PAD - PROMPT), (0, 0)))
    mine = (lax.broadcasted_iota(jnp.int32, (PAD, 1), 0) // BLOCK == member).astype(F32)
    scale = jnp.concatenate(
        [inverse, factor_rows[:, None], mine, jnp.zeros((PAD, LANES - 3), F32)], axis=1
    )
    parts = head_parts(grads, weights_all, along, act, base, cot, gain, scale, groups)
    parts = lax.all_to_all(
        parts.reshape(groups, BLOCK, width + LANES), mp, 0, 0, tiled=False
    )
    block = lambda array: lax.dynamic_slice_in_dim(array, member * BLOCK, BLOCK, 0)
    outgoing = prompt_grads(
        parts,
        block(act),
        base_mine,
        block(cot),
        gain,
        factor_cols[None, :],
        block(scale),
        group_size,
        pieces,
    )
    back = lax.all_to_all(outgoing, dp, 0, 0, tiled=False).astype(F32)
    reduced = jnp.sum(back[:, :, :own_cols], axis=0)
    low_picker = picker.astype(BF16)
    col_all = jnp.concatenate(
        [back[:, pieces : 2 * pieces, half:], back[:, :pieces, half:]], axis=2
    ).reshape(group_size, col_width)
    col_grad = dot(low_picker, col_all.astype(BF16), 0, 0)
    row_part = dot(back[:, 2 * pieces, half : half + BLOCK].astype(BF16), low_picker, 0, 0)
    both = lax.all_gather(jnp.concatenate([reduced, row_part], axis=1), mp, axis=0, tiled=True)
    both = both[:PROMPT].T
    prompt_grad = both[:own_cols].T
    row_grad = both[own_cols:]
    return (
        *adam_step(prompt_master, prompt_first, prompt_second, prompt_grad),
        *adam_step(row_factor, row_first, row_second, row_grad),
        *adam_step(col_factor, col_first, col_second, col_grad),
    )


def solution(mesh):
    ring = 4 if mesh.shape["dp"] % 4 == 0 else 2
    devices = mesh.devices.reshape(mesh.shape["dp"] // ring, ring, mesh.shape["mp"] // 2, 2)
    dp, mp = ROWS_AXES, HEADS_AXES
    return jax.shard_map(
        local,
        mesh=Mesh(devices, dp + mp),
        in_specs=(
            P(dp, None, None),
            P(),
            P(dp, mp),
            P(dp, mp),
            P(dp, mp),
            P(dp, None, mp),
            P(dp, None, None),
            P(None, dp),
            P(None, dp),
            P(None, dp),
            P(dp, None),
            P(dp, None),
            P(dp, None),
            P(dp, mp),
            P(dp, mp),
            P(dp, mp),
            P(dp),
            P(),
        ),
        out_specs=(
            P(None, dp),
            P(None, dp),
            P(None, dp),
            P(dp, None),
            P(dp, None),
            P(dp, None),
            P(dp, mp),
            P(dp, mp),
            P(dp, mp),
        ),
        check_vma=False,
    )
```

```python
import jax
import jax.numpy as jnp
from jax import lax
from jax.experimental import pallas as pl
from jax.experimental.pallas import tpu as pltpu
from jax.sharding import Mesh, PartitionSpec as P

HEAD_DIM = 64
PROMPT = 100
PAD = 128
BLOCK = 16
LANES = 128
HALF = 64
CHUNKS = 4

beta_first = 0.9
beta_second = 0.99
learn_rate = 0.01
adam_epsilon = 1e-08
norm_epsilon = 1e-06

ROWS_AXES = ("z", "y")
HEADS_AXES = ("x", "c")
BF16 = jnp.bfloat16
F32 = jnp.float32
VMEM = pl.BlockSpec(memory_space=pltpu.VMEM)
SMEM = pl.BlockSpec(memory_space=pltpu.SMEM)
PARAMS = pltpu.CompilerParams(vmem_limit_bytes=50 * 1024 * 1024)


def adam_step(param, moment_one, moment_two, gradient):
    first_new = beta_first * moment_one + (1.0 - beta_first) * gradient
    second_new = beta_second * moment_two + (1.0 - beta_second) * gradient * gradient
    return (
        param - learn_rate * first_new / (jnp.sqrt(second_new) + adam_epsilon),
        first_new,
        second_new,
    )


def dot(a, b, da, db, precision=None):
    return lax.dot_general(
        a, b, (((da,), (db,)), ((), ())), preferred_element_type=F32, precision=precision
    )


def iota(shape, axis):
    return lax.broadcasted_iota(jnp.int32, shape, axis)


def swap_halves(array):
    return jnp.concatenate([array[:, HALF:], array[:, :HALF]], axis=1)


def as_column(line):
    size = line.shape[1]
    eye = iota((size, size), 0) == iota((size, size), 1)
    return jnp.sum(jnp.where(eye, line, 0.0), axis=1, keepdims=True)


def factor_kernel(first_ref, slot_ref, row_ref, col_ref, out_ref):
    owned, width = col_ref.shape
    count = slot_ref.shape[1]
    pieces = width // LANES
    picker = (slot_ref[...] - first_ref[0] == iota((owned, count), 0)).astype(F32)
    high = lax.Precision.HIGHEST
    cols = dot(picker, col_ref[...], 0, 0, high)
    rows = dot(picker, row_ref[...], 0, 0, high)
    rows = jnp.concatenate([rows, jnp.zeros((count, LANES - PROMPT), F32)], axis=1)
    for piece in range(pieces):
        out_ref[:, piece, :] = cols[:, piece * LANES : (piece + 1) * LANES]
    out_ref[:, pieces, :] = rows
    for piece in range(pieces + 1, out_ref.shape[1]):
        out_ref[:, piece, :] = jnp.zeros((count, LANES), F32)


def main_kernel(
    place_ref,
    weight_hbm,
    hidden_ref,
    up_ref,
    cols_ref,
    rows_ref,
    gain_ref,
    cot_ref,
    keep_ref,
    send_ref,
    unit_out,
    base_out,
    scale_out,
    line_out,
    weights,
    base,
    unit,
    normed,
    total,
    qkv,
    parts,
    scale,
    sems,
):
    width = hidden_ref.shape[1]
    tokens = hidden_ref.shape[0]
    length = PAD + tokens
    inner = up_ref.shape[1]
    three = 3 * inner
    depth = width // CHUNKS
    groups = cols_ref.shape[0]
    size = width // groups
    pieces = size // LANES
    member = place_ref[0]
    core = place_ref[1]

    copies = [
        pltpu.make_async_copy(
            weight_hbm.at[pl.ds(k * depth, depth), :],
            weights.at[pl.ds(k * depth, depth), :],
            sems.at[k],
        )
        for k in range(CHUNKS)
    ]
    for copy in copies:
        copy.start()
    line = jnp.concatenate(
        [cols_ref[g, k : k + 1, :] for g in range(groups) for k in range(pieces)], axis=1
    )
    line_out[...] = line
    rows = as_column(rows_ref[...])
    own = pl.ds(pl.multiple_of(member * BLOCK, BLOCK), BLOCK)
    squares = jnp.zeros((PAD, 1), F32)
    for k in range(CHUNKS):
        copies[k].wait()
        span = slice(k * depth, (k + 1) * depth)
        part = dot(hidden_ref[:, span], weights[span, :three], 1, 0)
        if k == 0:
            total[...] = part
        elif k < CHUNKS - 1:
            total[...] += part
        else:
            qkv[PAD:, :] = (total[...] + part).astype(BF16)
        base_part = jnp.transpose(weights[span, three:].astype(F32))
        base[:, span] = base_part
        act = (base_part * rows * line[:, span]).astype(BF16).astype(F32)
        unit[:, span] = act
        squares = squares + jnp.sum(act * act, axis=1, keepdims=True)
    inverse = lax.rsqrt(squares * (1.0 / width) + norm_epsilon)
    scale[...] = jnp.where(iota((PAD, LANES), 1) == 0, inverse, rows)
    scale_own = scale[own, :]
    scale_out[...] = scale_own
    for k in range(CHUNKS):
        span = slice(k * depth, (k + 1) * depth)
        unit_part = unit[:, span] * inverse
        unit[:, span] = unit_part
        normed[:, span] = (unit_part * gain_ref[:, span]).astype(BF16)
    qkv[:PAD, :] = dot(normed[...], weights[:, :three], 1, 0).astype(BF16)

    column = iota((length, length), 1)
    real_key = (column < PROMPT) | (column >= PAD)
    along = jnp.zeros((PAD, 1), F32)
    grads = [[], [], []]
    for head in range(inner // HEAD_DIM):
        at = head * HEAD_DIM
        query = qkv[:, at : at + HEAD_DIM]
        key = qkv[:, inner + at : inner + at + HEAD_DIM]
        value = qkv[:, 2 * inner + at : 2 * inner + at + HEAD_DIM]
        up = up_ref[:, at : at + HEAD_DIM]
        exponent = jnp.where(real_key, jnp.exp(dot(query, key, 1, 1)), 0.0)
        attend = exponent / jnp.sum(exponent, axis=1, keepdims=True)
        grad_prob = dot(up, value, 1, 1)
        row_dot = jnp.sum(attend * grad_prob, axis=1, keepdims=True)
        grad_score = (attend * (grad_prob - row_dot)).astype(BF16)
        found = (
            dot(grad_score[:PAD, :], key, 1, 0).astype(BF16),
            dot(grad_score[:, :PAD], query, 0, 0).astype(BF16),
            dot(attend[:, :PAD].astype(BF16), up, 0, 0).astype(BF16),
        )
        for kind, (grad, low) in enumerate(zip(found, (query, key, value))):
            grads[kind].append(grad)
            along = along + jnp.sum(
                grad.astype(F32) * low[:PAD].astype(F32), axis=1, keepdims=True
            )
    grad_all = jnp.concatenate(grads[0] + grads[1] + grads[2], axis=1)

    mean = along * (1.0 / width)
    strength = inverse * rows
    for g in range(groups):
        span = slice(g * size, (g + 1) * size)
        part = dot(grad_all, weights[span, :three], 1, 1)
        parts[:, span] = part
        weighted = base[:, span] * strength
        base_own = base[own, span]
        base_out[:, span] = base_own
        unit_out[:, span] = unit[own, span]
        cols = (
            gain_ref[:, span] * jnp.sum(part * weighted, axis=0, keepdims=True)
            - jnp.sum(weighted * unit[:, span] * mean, axis=0, keepdims=True)
            + jnp.sum(
                cot_ref[:, span].astype(F32) * base_own * scale_own[:, 1:2], axis=0, keepdims=True
            )
        )
        parts[g * BLOCK : (g + 1) * BLOCK, width:] = jnp.concatenate(
            [cols[:, at : at + LANES] for at in range(0, size, LANES)]
            + [jnp.zeros((BLOCK - pieces, LANES), F32)],
            axis=0,
        )
    for pair in range(groups // 2):
        start = pl.multiple_of((2 * pair + core) * BLOCK, BLOCK)
        keep_ref[pair, :, :] = parts[pl.ds(start, BLOCK), :]
        start = pl.multiple_of((2 * pair + 1 - core) * BLOCK, BLOCK)
        send_ref[pair, :, :] = parts[pl.ds(start, BLOCK), :]


def main_part(place, weights, hidden, up, cols, rows, gain, cot):
    width = hidden.shape[1]
    length = PAD + hidden.shape[0]
    three = 3 * up.shape[1]
    groups = cols.shape[0]
    half = jax.ShapeDtypeStruct((groups // 2, BLOCK, width + LANES), F32)
    own = jax.ShapeDtypeStruct((BLOCK, width), F32)
    return pl.pallas_call(
        main_kernel,
        out_shape=(
            half,
            half,
            own,
            own,
            jax.ShapeDtypeStruct((BLOCK, LANES), F32),
            jax.ShapeDtypeStruct((1, width), F32),
        ),
        in_specs=[SMEM, pl.BlockSpec(memory_space=pl.ANY)] + [VMEM] * 6,
        out_specs=(VMEM,) * 6,
        scratch_shapes=[
            pltpu.VMEM(weights.shape, BF16),
            pltpu.VMEM((PAD, width), F32),
            pltpu.VMEM((PAD, width), F32),
            pltpu.VMEM((PAD, width), BF16),
            pltpu.VMEM((length - PAD, three), F32),
            pltpu.VMEM((length, three), BF16),
            pltpu.VMEM((PAD, width + LANES), F32),
            pltpu.VMEM((PAD, LANES), F32),
            pltpu.SemaphoreType.DMA((CHUNKS,)),
        ],
        compiler_params=PARAMS,
    )(place, weights, hidden, up, cols, rows, gain, cot)


def prompt_kernel(pieces, got_ref, unit_ref, base_ref, cot_ref, gain_ref, cols_ref, scale_ref, out_ref):
    width = unit_ref.shape[1]
    total = got_ref[0, :, :].astype(F32)
    for source in range(1, got_ref.shape[0]):
        total = total + got_ref[source, :, :].astype(F32)
    inverse = scale_ref[:, 0:1]
    rows = scale_ref[:, 1:2]
    unit = unit_ref[...]
    scaled = total[:, :width] * gain_ref[...]
    mean = jnp.sum(scaled * unit, axis=1, keepdims=True) * (1.0 / width)
    grad = cot_ref[...].astype(F32) + inverse * (scaled - unit * mean)
    times_cols = grad * cols_ref[...]
    grad_rows = jnp.sum(times_cols * base_ref[...], axis=1, keepdims=True)
    grad_base = times_cols * rows
    cols = total[:pieces, width:]
    spare = BLOCK - 2 * pieces
    line = jnp.sum(
        jnp.where(iota((BLOCK, LANES), 1) == iota((BLOCK, LANES), 0) + HALF, grad_rows, 0.0),
        axis=0,
        keepdims=True,
    )
    under = jnp.where(iota((spare, LANES), 0) == 0, line, 0.0)
    tail = jnp.concatenate([cols, swap_halves(cols), under], axis=0)
    first_half = iota((BLOCK, LANES), 1) < HALF
    for pair in range(width // LANES):
        block = grad_base[:, pair * LANES : (pair + 1) * LANES]
        out_ref[2 * pair, :, :] = jnp.where(first_half, block, tail).astype(BF16)
        out_ref[2 * pair + 1, :, :] = jnp.where(first_half, swap_halves(block), tail).astype(BF16)


def owner_kernel(first_ref, slot_ref, back_ref, shared_ref, col_ref):
    owned, width = col_ref.shape
    count = slot_ref.shape[1]
    pieces = width // LANES
    picker = (slot_ref[...] - first_ref[0] == iota((owned, count), 0)).astype(BF16)
    back = back_ref[...].astype(F32)
    total = jnp.sum(back, axis=0)
    first_half = iota((owned, LANES), 1) < HALF
    for piece in range(pieces):
        upper = dot(picker, back[:, piece, :].astype(BF16), 1, 0)
        lower = dot(picker, back[:, pieces + piece, :].astype(BF16), 1, 0)
        col_ref[:, piece * LANES : (piece + 1) * LANES] = jnp.where(
            first_half, swap_halves(lower), upper
        )
    rows = dot(back[:, 2 * pieces, :].astype(BF16), picker, 0, 1)
    shared_ref[...] = jnp.concatenate([total[:, :HALF], rows[HALF : HALF + BLOCK, :]], axis=1)


def update_kernel(grads_ref, *refs):
    grads = jnp.transpose(grads_ref[...])
    for kind in range(2):
        param, one, two, param_out, one_out, two_out = refs[kind::2]
        rows = param.shape[0]
        found = grads[kind * HALF : kind * HALF + rows, : param.shape[1]]
        param_out[...], one_out[...], two_out[...] = adam_step(param[...], one[...], two[...], found)


def local(
    hidden_rows,
    norm_gain,
    w_query,
    w_key,
    w_value,
    head_cotangent,
    prompt_cotangent,
    prompt_master,
    prompt_first,
    prompt_second,
    row_factor,
    row_first,
    row_second,
    col_factor,
    col_first,
    col_second,
    row_tenant,
    tenant_slot,
):
    dp, mp = ROWS_AXES, HEADS_AXES
    count = lax.axis_size(dp)
    groups = lax.axis_size(mp)
    device = lax.axis_index(dp)
    member = lax.axis_index(mp)
    owned, col_width = col_factor.shape
    width = hidden_rows.shape[2]
    pieces = col_width // LANES
    padding = ((0, 0), (0, LANES - PROMPT))

    weights = jnp.concatenate(
        [w_query, w_key, w_value, jnp.pad(prompt_master.T.astype(BF16), padding)], axis=1
    )
    weights = lax.all_gather(weights, "y", axis=0, tiled=True)
    slot = lax.dynamic_index_in_dim(tenant_slot, row_tenant[0], 0, keepdims=False)
    weights, slot = lax.optimization_barrier((weights, slot))
    weights = lax.all_gather(weights, "z", axis=0, tiled=True)

    slots = lax.psum(jnp.where(lax.iota(jnp.int32, count) == device, slot, 0), dp)[None, :]
    first = (device * owned).astype(jnp.int32).reshape(1)
    terms = pl.pallas_call(
        factor_kernel,
        out_shape=jax.ShapeDtypeStruct((count, 8, LANES), F32),
        in_specs=[SMEM, VMEM, VMEM, VMEM],
        out_specs=VMEM,
        compiler_params=PARAMS,
    )(first, slots, row_factor, col_factor)
    terms = jnp.sum(lax.all_to_all(terms, dp, 0, 0, tiled=False), axis=0)
    factor_cols = lax.all_to_all(
        jnp.broadcast_to(terms[None], (groups, 8, LANES)), mp, 0, 0, tiled=False
    )
    factor_rows = terms[pieces : pieces + 1]

    gain = norm_gain[None, :]
    hidden = hidden_rows[0].astype(F32)
    inverse = lax.rsqrt(jnp.mean(hidden * hidden, axis=-1, keepdims=True) + norm_epsilon)
    hidden = (hidden * inverse * gain).astype(BF16)
    upstream = jnp.concatenate(
        [
            jnp.pad(head_cotangent[0, :PROMPT], ((0, PAD - PROMPT), (0, 0))),
            head_cotangent[0, PROMPT:],
        ],
        axis=0,
    )
    cot = lax.dynamic_slice_in_dim(
        jnp.pad(prompt_cotangent[0], ((0, PAD - PROMPT), (0, 0))), member * BLOCK, BLOCK, 0
    )
    place = jnp.stack([member, lax.axis_index("c")]).astype(jnp.int32)
    keep, send, unit_own, base_own, scale_own, line = main_part(
        place, weights, hidden, upstream, factor_cols, factor_rows, gain, cot
    )

    parts = (keep + lax.ppermute(send, "c", [(0, 1), (1, 0)])).astype(BF16)
    parts = lax.all_to_all(parts, "x", 0, 0, tiled=False)
    outgoing = pl.pallas_call(
        lambda *refs: prompt_kernel(pieces, *refs),
        out_shape=jax.ShapeDtypeStruct((count, BLOCK, LANES), BF16),
        in_specs=[VMEM] * 7,
        out_specs=VMEM,
        compiler_params=PARAMS,
    )(parts, unit_own, base_own, cot, gain, line, scale_own)

    back = lax.all_to_all(outgoing, dp, 0, 0, tiled=False)
    shared, col_grad = pl.pallas_call(
        owner_kernel,
        out_shape=(
            jax.ShapeDtypeStruct((BLOCK, LANES), F32),
            jax.ShapeDtypeStruct((owned, col_width), F32),
        ),
        in_specs=[SMEM, VMEM, VMEM],
        out_specs=(VMEM, VMEM),
        compiler_params=PARAMS,
    )(first, slots, back)
    shared = lax.all_to_all(
        jnp.broadcast_to(shared[None], (groups, BLOCK, LANES)), mp, 0, 0, tiled=False
    ).reshape(PAD, LANES)
    operands = [
        part
        for pair in zip(
            (prompt_master.T, prompt_first.T, prompt_second.T), (row_factor, row_first, row_second)
        )
        for part in pair
    ]
    new = pl.pallas_call(
        update_kernel,
        out_shape=tuple(jax.ShapeDtypeStruct(part.shape, F32) for part in operands),
        in_specs=[VMEM] * 7,
        out_specs=(VMEM,) * 6,
        compiler_params=PARAMS,
    )(shared, *operands)
    return (
        *(part.T for part in new[0::2]),
        *new[1::2],
        *adam_step(col_factor, col_first, col_second, col_grad),
    )


def solution(mesh):
    ring = 4 if mesh.shape["dp"] % 4 == 0 else 2
    devices = mesh.devices.reshape(mesh.shape["dp"] // ring, ring, mesh.shape["mp"] // 2, 2)
    dp, mp = ROWS_AXES, HEADS_AXES
    return jax.shard_map(
        local,
        mesh=Mesh(devices, dp + mp),
        in_specs=(
            P(dp, None, None),
            P(),
            P(dp, mp),
            P(dp, mp),
            P(dp, mp),
            P(dp, None, mp),
            P(dp, None, None),
            P(None, dp),
            P(None, dp),
            P(None, dp),
            P(dp, None),
            P(dp, None),
            P(dp, None),
            P(dp, mp),
            P(dp, mp),
            P(dp, mp),
            P(dp),
            P(),
        ),
        out_specs=(
            P(None, dp),
            P(None, dp),
            P(None, dp),
            P(dp, None),
            P(dp, None),
            P(dp, None),
            P(dp, mp),
            P(dp, mp),
            P(dp, mp),
        ),
        check_vma=False,
    )
```

```python
import jax
import jax.numpy as jnp
from jax import lax
from jax.experimental import pallas as pl
from jax.experimental.pallas import tpu as pltpu
from jax.sharding import Mesh, PartitionSpec as P

HEAD_DIM = 64
PROMPT = 100
PAD = 128
BLOCK = 16
LANES = 128
HALF = 64
CHUNKS = 4

beta_first = 0.9
beta_second = 0.99
learn_rate = 0.01
adam_epsilon = 1e-08
norm_epsilon = 1e-06

ROWS_AXES = ("z", "y")
HEADS_AXES = ("x", "c")
BF16 = jnp.bfloat16
F32 = jnp.float32
VMEM = pl.BlockSpec(memory_space=pltpu.VMEM)
SMEM = pl.BlockSpec(memory_space=pltpu.SMEM)
PARAMS = pltpu.CompilerParams(vmem_limit_bytes=50 * 1024 * 1024)


def adam_step(param, moment_one, moment_two, gradient):
    first_new = beta_first * moment_one + (1.0 - beta_first) * gradient
    second_new = beta_second * moment_two + (1.0 - beta_second) * gradient * gradient
    return (
        param - learn_rate * first_new / (jnp.sqrt(second_new) + adam_epsilon),
        first_new,
        second_new,
    )


def dot(a, b, da, db, precision=None):
    return lax.dot_general(
        a, b, (((da,), (db,)), ((), ())), preferred_element_type=F32, precision=precision
    )


def iota(shape, axis):
    return lax.broadcasted_iota(jnp.int32, shape, axis)


def swap_halves(array):
    return jnp.concatenate([array[:, HALF:], array[:, :HALF]], axis=1)


def as_column(line):
    size = line.shape[1]
    eye = iota((size, size), 0) == iota((size, size), 1)
    return jnp.sum(jnp.where(eye, line, 0.0), axis=1, keepdims=True)


def factor_kernel(first_ref, slot_ref, row_ref, col_ref, out_ref):
    owned, width = col_ref.shape
    count = slot_ref.shape[1]
    pieces = width // LANES
    picker = (slot_ref[...] - first_ref[0] == iota((owned, count), 0)).astype(F32)
    high = lax.Precision.HIGHEST
    cols = dot(picker, col_ref[...], 0, 0, high)
    rows = dot(picker, row_ref[...], 0, 0, high)
    rows = jnp.concatenate([rows, jnp.zeros((count, LANES - PROMPT), F32)], axis=1)
    for piece in range(pieces):
        out_ref[:, piece, :] = cols[:, piece * LANES : (piece + 1) * LANES]
    out_ref[:, pieces, :] = rows
    for piece in range(pieces + 1, out_ref.shape[1]):
        out_ref[:, piece, :] = jnp.zeros((count, LANES), F32)


def main_kernel(
    place_ref,
    pair_hbm,
    own_hbm,
    left_hbm,
    right_hbm,
    far_first_hbm,
    far_second_hbm,
    hidden_ref,
    up_ref,
    cols_ref,
    rows_ref,
    gain_ref,
    cot_ref,
    keep_ref,
    send_ref,
    unit_out,
    base_out,
    scale_out,
    line_out,
    pair,
    single,
    base,
    unit,
    normed,
    total,
    qkv,
    parts,
    scale,
    sems,
):
    width = hidden_ref.shape[1]
    tokens = hidden_ref.shape[0]
    length = PAD + tokens
    inner = up_ref.shape[1]
    depth = width // CHUNKS
    groups = cols_ref.shape[0]
    size = width // groups
    pieces = size // LANES
    member = place_ref[0]
    core = place_ref[1]

    half = single.shape[0] // 2
    copies = [
        pltpu.make_async_copy(own_hbm, single.at[:, place_ref[2]], sems.at[0]),
        pltpu.make_async_copy(left_hbm, single.at[:, place_ref[3]], sems.at[1]),
        pltpu.make_async_copy(right_hbm, single.at[:, place_ref[4]], sems.at[2]),
        pltpu.make_async_copy(far_first_hbm, single.at[:half, place_ref[5]], sems.at[3]),
        pltpu.make_async_copy(far_second_hbm, single.at[half:, place_ref[5]], sems.at[4]),
    ] + [
        pltpu.make_async_copy(
            pair_hbm.at[pl.ds(k * depth, depth), :],
            pair.at[pl.ds(k * depth, depth), :],
            sems.at[5 + k],
        )
        for k in range(CHUNKS)
    ]
    for copy in copies:
        copy.start()
    line = jnp.concatenate(
        [cols_ref[g, k : k + 1, :] for g in range(groups) for k in range(pieces)], axis=1
    )
    line_out[...] = line
    rows = as_column(rows_ref[...])
    own = pl.ds(pl.multiple_of(member * BLOCK, BLOCK), BLOCK)
    squares = jnp.zeros((PAD, 1), F32)
    for k in range(5):
        copies[k].wait()
    lead = single.shape[0] // CHUNKS
    single_part = lambda k, start, stop: single[
        k * lead : (k + 1) * lead, :, :, start:stop
    ].reshape(depth, stop - start)
    for k in range(CHUNKS):
        span = slice(k * depth, (k + 1) * depth)
        base_part = jnp.transpose(single_part(k, inner, inner + LANES).astype(F32))
        base[:, span] = base_part
        act = (base_part * rows * line[:, span]).astype(BF16).astype(F32)
        unit[:, span] = act
        squares = squares + jnp.sum(act * act, axis=1, keepdims=True)
    inverse = lax.rsqrt(squares * (1.0 / width) + norm_epsilon)
    scale[...] = jnp.where(iota((PAD, LANES), 1) == 0, inverse, rows)
    scale_own = scale[own, :]
    scale_out[...] = scale_own
    for k in range(CHUNKS):
        span = slice(k * depth, (k + 1) * depth)
        unit_part = unit[:, span] * inverse
        unit[:, span] = unit_part
        normed[:, span] = (unit_part * gain_ref[:, span]).astype(BF16)
    query_weights = single[:, :, :, :inner].reshape(width, inner)
    qkv[PAD:, :inner] = dot(hidden_ref[...], query_weights, 1, 0).astype(BF16)
    qkv[:PAD, :inner] = dot(normed[...], query_weights, 1, 0).astype(BF16)
    for k in range(CHUNKS):
        copies[5 + k].wait()
        span = slice(k * depth, (k + 1) * depth)
        part = dot(hidden_ref[:, span], pair[span, :], 1, 0)
        if k == 0:
            total[...] = part
        elif k < CHUNKS - 1:
            total[...] += part
        else:
            qkv[PAD:, inner:] = (total[...] + part).astype(BF16)
    qkv[:PAD, inner:] = dot(normed[...], pair[...], 1, 0).astype(BF16)

    column = iota((length, length), 1)
    real_key = (column < PROMPT) | (column >= PAD)
    along = jnp.zeros((PAD, 1), F32)
    grads = [[], [], []]
    for head in range(inner // HEAD_DIM):
        at = head * HEAD_DIM
        query = qkv[:, at : at + HEAD_DIM]
        key = qkv[:, inner + at : inner + at + HEAD_DIM]
        value = qkv[:, 2 * inner + at : 2 * inner + at + HEAD_DIM]
        up = up_ref[:, at : at + HEAD_DIM]
        exponent = jnp.where(real_key, jnp.exp(dot(query, key, 1, 1)), 0.0)
        attend = exponent / jnp.sum(exponent, axis=1, keepdims=True)
        grad_prob = dot(up, value, 1, 1)
        row_dot = jnp.sum(attend * grad_prob, axis=1, keepdims=True)
        grad_score = (attend * (grad_prob - row_dot)).astype(BF16)
        found = (
            dot(grad_score[:PAD, :], key, 1, 0).astype(BF16),
            dot(grad_score[:, :PAD], query, 0, 0).astype(BF16),
            dot(attend[:, :PAD].astype(BF16), up, 0, 0).astype(BF16),
        )
        for kind, (grad, low) in enumerate(zip(found, (query, key, value))):
            grads[kind].append(grad)
            along = along + jnp.sum(
                grad.astype(F32) * low[:PAD].astype(F32), axis=1, keepdims=True
            )
    grad_all = jnp.concatenate(grads[0] + grads[1] + grads[2], axis=1)

    mean = along * (1.0 / width)
    strength = inverse * rows
    for g in range(groups):
        span = slice(g * size, (g + 1) * size)
        place = slice(g * single.shape[0] // groups, (g + 1) * single.shape[0] // groups)
        part = dot(grad_all[:, :inner], single[place, :, :, :inner].reshape(size, inner), 1, 1)
        part = part + dot(grad_all[:, inner:], pair[span, :], 1, 1)
        parts[:, span] = part
        weighted = base[:, span] * strength
        base_own = base[own, span]
        base_out[:, span] = base_own
        unit_out[:, span] = unit[own, span]
        cols = (
            gain_ref[:, span] * jnp.sum(part * weighted, axis=0, keepdims=True)
            - jnp.sum(weighted * unit[:, span] * mean, axis=0, keepdims=True)
            + jnp.sum(
                cot_ref[:, span].astype(F32) * base_own * scale_own[:, 1:2], axis=0, keepdims=True
            )
        )
        parts[g * BLOCK : (g + 1) * BLOCK, width:] = jnp.concatenate(
            [cols[:, at : at + LANES] for at in range(0, size, LANES)]
            + [jnp.zeros((BLOCK - pieces, LANES), F32)],
            axis=0,
        )
    for pair in range(groups // 2):
        start = pl.multiple_of((2 * pair + core) * BLOCK, BLOCK)
        keep_ref[pair, :, :] = parts[pl.ds(start, BLOCK), :]
        start = pl.multiple_of((2 * pair + 1 - core) * BLOCK, BLOCK)
        send_ref[pair, :, :] = parts[pl.ds(start, BLOCK), :]


def main_part(place, pair, singles, hidden, up, cols, rows, gain, cot):
    width = hidden.shape[1]
    length = PAD + hidden.shape[0]
    inner = up.shape[1]
    ring = width // (singles[0].shape[0] * singles[0].shape[1])
    groups = cols.shape[0]
    half = jax.ShapeDtypeStruct((groups // 2, BLOCK, width + LANES), F32)
    own = jax.ShapeDtypeStruct((BLOCK, width), F32)
    return pl.pallas_call(
        main_kernel,
        out_shape=(
            half,
            half,
            own,
            own,
            jax.ShapeDtypeStruct((BLOCK, LANES), F32),
            jax.ShapeDtypeStruct((1, width), F32),
        ),
        in_specs=[SMEM] + [pl.BlockSpec(memory_space=pl.ANY)] * 6 + [VMEM] * 6,
        out_specs=(VMEM,) * 6,
        scratch_shapes=[
            pltpu.VMEM(pair.shape, BF16),
            pltpu.VMEM((singles[0].shape[0], ring) + singles[0].shape[1:], BF16),
            pltpu.VMEM((PAD, width), F32),
            pltpu.VMEM((PAD, width), F32),
            pltpu.VMEM((PAD, width), BF16),
            pltpu.VMEM((length - PAD, 2 * inner), F32),
            pltpu.VMEM((length, 3 * inner), BF16),
            pltpu.VMEM((PAD, width + LANES), F32),
            pltpu.VMEM((PAD, LANES), F32),
            pltpu.SemaphoreType.DMA((5 + CHUNKS,)),
        ],
        compiler_params=PARAMS,
    )(place, pair, *singles, hidden, up, cols, rows, gain, cot)


def prompt_kernel(pieces, got_ref, unit_ref, base_ref, cot_ref, gain_ref, cols_ref, scale_ref, out_ref):
    width = unit_ref.shape[1]
    total = got_ref[0, :, :].astype(F32)
    for source in range(1, got_ref.shape[0]):
        total = total + got_ref[source, :, :].astype(F32)
    inverse = scale_ref[:, 0:1]
    rows = scale_ref[:, 1:2]
    unit = unit_ref[...]
    scaled = total[:, :width] * gain_ref[...]
    mean = jnp.sum(scaled * unit, axis=1, keepdims=True) * (1.0 / width)
    grad = cot_ref[...].astype(F32) + inverse * (scaled - unit * mean)
    times_cols = grad * cols_ref[...]
    grad_rows = jnp.sum(times_cols * base_ref[...], axis=1, keepdims=True)
    grad_base = times_cols * rows
    cols = total[:pieces, width:]
    spare = BLOCK - 2 * pieces
    line = jnp.sum(
        jnp.where(iota((BLOCK, LANES), 1) == iota((BLOCK, LANES), 0) + HALF, grad_rows, 0.0),
        axis=0,
        keepdims=True,
    )
    under = jnp.where(iota((spare, LANES), 0) == 0, line, 0.0)
    tail = jnp.concatenate([cols, swap_halves(cols), under], axis=0)
    first_half = iota((BLOCK, LANES), 1) < HALF
    for pair in range(width // LANES):
        block = grad_base[:, pair * LANES : (pair + 1) * LANES]
        out_ref[2 * pair, :, :] = jnp.where(first_half, block, tail).astype(BF16)
        out_ref[2 * pair + 1, :, :] = jnp.where(first_half, swap_halves(block), tail).astype(BF16)


def owner_kernel(first_ref, slot_ref, back_ref, shared_ref, col_ref):
    owned, width = col_ref.shape
    count = slot_ref.shape[1]
    pieces = width // LANES
    picker = (slot_ref[...] - first_ref[0] == iota((owned, count), 0)).astype(BF16)
    back = back_ref[...].astype(F32)
    total = jnp.sum(back, axis=0)
    first_half = iota((owned, LANES), 1) < HALF
    for piece in range(pieces):
        upper = dot(picker, back[:, piece, :].astype(BF16), 1, 0)
        lower = dot(picker, back[:, pieces + piece, :].astype(BF16), 1, 0)
        col_ref[:, piece * LANES : (piece + 1) * LANES] = jnp.where(
            first_half, swap_halves(lower), upper
        )
    rows = dot(back[:, 2 * pieces, :].astype(BF16), picker, 0, 1)
    shared_ref[...] = jnp.concatenate([total[:, :HALF], rows[HALF : HALF + BLOCK, :]], axis=1)


def update_kernel(grads_ref, *refs):
    grads = jnp.transpose(grads_ref[...])
    for kind in range(2):
        param, one, two, param_out, one_out, two_out = refs[kind::2]
        rows = param.shape[0]
        found = grads[kind * HALF : kind * HALF + rows, : param.shape[1]]
        param_out[...], one_out[...], two_out[...] = adam_step(param[...], one[...], two[...], found)


def local(
    hidden_rows,
    norm_gain,
    w_query,
    w_key,
    w_value,
    head_cotangent,
    prompt_cotangent,
    prompt_master,
    prompt_first,
    prompt_second,
    row_factor,
    row_first,
    row_second,
    col_factor,
    col_first,
    col_second,
    row_tenant,
    tenant_slot,
):
    dp, mp = ROWS_AXES, HEADS_AXES
    count = lax.axis_size(dp)
    groups = lax.axis_size(mp)
    device = lax.axis_index(dp)
    member = lax.axis_index(mp)
    owned, col_width = col_factor.shape
    width = hidden_rows.shape[2]
    pieces = col_width // LANES

    depth = w_query.shape[0]
    inner = w_query.shape[1]
    ring = lax.axis_size("y")
    slot = lax.dynamic_index_in_dim(tenant_slot, row_tenant[0], 0, keepdims=False)
    marks = jnp.stack([slot // owned, slot % owned]).astype(BF16)
    marks = jnp.broadcast_to(jnp.pad(marks, (0, LANES - 2))[None], (depth, LANES))
    pair = lax.all_gather(jnp.concatenate([w_key, w_value, marks], axis=1), "y", axis=0, tiled=True)
    marks = pair.reshape(ring, depth, -1)[:, 0, 2 * inner : 2 * inner + 2].reshape(-1)
    pair = pair[:, : 2 * inner]

    marks = jnp.broadcast_to(
        jnp.pad(marks, (0, LANES - PROMPT - marks.shape[0]))[None], (depth, LANES - PROMPT)
    )
    own = jnp.concatenate([w_query, prompt_master.T.astype(BF16), marks], axis=1)
    pair, own = lax.optimization_barrier((pair, own))
    pair = lax.all_gather(pair, "z", axis=0, tiled=True)
    own = lax.all_gather(own, "z", axis=0, tiled=False)
    half = own.shape[0] // 2
    up_ring = [(i, (i + 1) % ring) for i in range(ring)]
    down_ring = [(i, (i - 1) % ring) for i in range(ring)]
    left = lax.ppermute(own, "y", up_ring)
    right = lax.ppermute(own, "y", down_ring)
    far_first = lax.ppermute(left[:half], "y", up_ring)
    far_second = lax.ppermute(right[half:], "y", down_ring)
    singles = (own, left, right, far_first, far_second)

    marks = own[:, 0, inner + PROMPT : inner + PROMPT + 2 * ring].reshape(count, 2)
    marks = marks.astype(jnp.int32)
    slots = (marks[:, 0] * owned + marks[:, 1])[None, :]
    first = (device * owned).astype(jnp.int32).reshape(1)
    terms = pl.pallas_call(
        factor_kernel,
        out_shape=jax.ShapeDtypeStruct((count, 8, LANES), F32),
        in_specs=[SMEM, VMEM, VMEM, VMEM],
        out_specs=VMEM,
        compiler_params=PARAMS,
    )(first, slots, row_factor, col_factor)
    terms = jnp.sum(lax.all_to_all(terms, dp, 0, 0, tiled=False), axis=0)
    factor_cols = lax.all_to_all(
        jnp.broadcast_to(terms[None], (groups, 8, LANES)), mp, 0, 0, tiled=False
    )
    factor_rows = terms[pieces : pieces + 1]

    gain = norm_gain[None, :]
    hidden = hidden_rows[0].astype(F32)
    inverse = lax.rsqrt(jnp.mean(hidden * hidden, axis=-1, keepdims=True) + norm_epsilon)
    hidden = (hidden * inverse * gain).astype(BF16)
    upstream = jnp.concatenate(
        [
            jnp.pad(head_cotangent[0, :PROMPT], ((0, PAD - PROMPT), (0, 0))),
            head_cotangent[0, PROMPT:],
        ],
        axis=0,
    )
    cot = lax.dynamic_slice_in_dim(
        jnp.pad(prompt_cotangent[0], ((0, PAD - PROMPT), (0, 0))), member * BLOCK, BLOCK, 0
    )
    y = lax.axis_index("y")
    place = jnp.stack(
        [member, lax.axis_index("c"), y, (y - 1) % ring, (y + 1) % ring, (y + 2) % ring]
    ).astype(jnp.int32)
    keep, send, unit_own, base_own, scale_own, line = main_part(
        place, pair, singles, hidden, upstream, factor_cols, factor_rows, gain, cot
    )

    parts = (keep + lax.ppermute(send, "c", [(0, 1), (1, 0)])).astype(BF16)
    parts = lax.all_to_all(parts, "x", 0, 0, tiled=False)
    outgoing = pl.pallas_call(
        lambda *refs: prompt_kernel(pieces, *refs),
        out_shape=jax.ShapeDtypeStruct((count, BLOCK, LANES), BF16),
        in_specs=[VMEM] * 7,
        out_specs=VMEM,
        compiler_params=PARAMS,
    )(parts, unit_own, base_own, cot, gain, line, scale_own)

    back = lax.all_to_all(outgoing, dp, 0, 0, tiled=False)
    shared, col_grad = pl.pallas_call(
        owner_kernel,
        out_shape=(
            jax.ShapeDtypeStruct((BLOCK, LANES), F32),
            jax.ShapeDtypeStruct((owned, col_width), F32),
        ),
        in_specs=[SMEM, VMEM, VMEM],
        out_specs=(VMEM, VMEM),
        compiler_params=PARAMS,
    )(first, slots, back)
    shared = lax.all_to_all(
        jnp.broadcast_to(shared[None], (groups, BLOCK, LANES)), mp, 0, 0, tiled=False
    ).reshape(PAD, LANES)
    operands = [
        part
        for pair in zip(
            (prompt_master.T, prompt_first.T, prompt_second.T), (row_factor, row_first, row_second)
        )
        for part in pair
    ]
    new = pl.pallas_call(
        update_kernel,
        out_shape=tuple(jax.ShapeDtypeStruct(part.shape, F32) for part in operands),
        in_specs=[VMEM] * 7,
        out_specs=(VMEM,) * 6,
        compiler_params=PARAMS,
    )(shared, *operands)
    return (
        *(part.T for part in new[0::2]),
        *new[1::2],
        *adam_step(col_factor, col_first, col_second, col_grad),
    )


def solution(mesh):
    ring = 4 if mesh.shape["dp"] % 4 == 0 else 2
    devices = mesh.devices.reshape(mesh.shape["dp"] // ring, ring, mesh.shape["mp"] // 2, 2)
    dp, mp = ROWS_AXES, HEADS_AXES
    return jax.shard_map(
        local,
        mesh=Mesh(devices, dp + mp),
        in_specs=(
            P(dp, None, None),
            P(),
            P(dp, mp),
            P(dp, mp),
            P(dp, mp),
            P(dp, None, mp),
            P(dp, None, None),
            P(None, dp),
            P(None, dp),
            P(None, dp),
            P(dp, None),
            P(dp, None),
            P(dp, None),
            P(dp, mp),
            P(dp, mp),
            P(dp, mp),
            P(dp),
            P(),
        ),
        out_specs=(
            P(None, dp),
            P(None, dp),
            P(None, dp),
            P(dp, None),
            P(dp, None),
            P(dp, None),
            P(dp, mp),
            P(dp, mp),
            P(dp, mp),
        ),
        check_vma=False,
    )
```

```python
import jax
import jax.numpy as jnp
from jax import lax
from jax.experimental import pallas as pl
from jax.experimental.pallas import tpu as pltpu
from jax.sharding import Mesh, PartitionSpec as P

HEAD_DIM = 64
PROMPT = 100
PAD = 128
BLOCK = 16
LANES = 128
HALF = 64
CHUNKS = 4

beta_first = 0.9
beta_second = 0.99
learn_rate = 0.01
adam_epsilon = 1e-08
norm_epsilon = 1e-06

ROWS_AXES = ("z", "y")
HEADS_AXES = ("x", "c")
BF16 = jnp.bfloat16
F32 = jnp.float32
VMEM = pl.BlockSpec(memory_space=pltpu.VMEM)
SMEM = pl.BlockSpec(memory_space=pltpu.SMEM)
PARAMS = pltpu.CompilerParams(vmem_limit_bytes=16 * 1024 * 1024)
MAIN_PARAMS = pltpu.CompilerParams(vmem_limit_bytes=32 * 1024 * 1024)


def adam_step(param, moment_one, moment_two, gradient):
    first_new = beta_first * moment_one + (1.0 - beta_first) * gradient
    second_new = beta_second * moment_two + (1.0 - beta_second) * gradient * gradient
    return (
        param - learn_rate * first_new / (jnp.sqrt(second_new) + adam_epsilon),
        first_new,
        second_new,
    )


def dot(a, b, da, db, precision=None):
    return lax.dot_general(
        a, b, (((da,), (db,)), ((), ())), preferred_element_type=F32, precision=precision
    )


def iota(shape, axis):
    return lax.broadcasted_iota(jnp.int32, shape, axis)


def swap_halves(array):
    return jnp.concatenate([array[:, HALF:], array[:, :HALF]], axis=1)


def as_column(line):
    size = line.shape[1]
    eye = iota((size, size), 0) == iota((size, size), 1)
    return jnp.sum(jnp.where(eye, line, 0.0), axis=1, keepdims=True)


def lead_kernel(owned, tenant_ref, slot_ref, key_ref, value_ref, out_ref):
    depth, inner = key_ref.shape
    slot = slot_ref[tenant_ref[0]]
    owner = lax.div(slot, owned)
    lane = iota((depth, LANES), 1)
    marks = jnp.where(lane == 0, owner, jnp.where(lane == 1, slot - owner * owned, 0))
    out_ref[:, :inner] = key_ref[...]
    out_ref[:, inner : 2 * inner] = value_ref[...]
    out_ref[:, 2 * inner :] = marks.astype(F32).astype(BF16)


def factor_kernel(first_ref, slot_ref, row_ref, col_ref, out_ref):
    owned, width = col_ref.shape
    count = slot_ref.shape[1]
    pieces = width // LANES
    picker = (slot_ref[...] - first_ref[0] == iota((owned, count), 0)).astype(F32)
    high = lax.Precision.HIGHEST
    cols = dot(picker, col_ref[...], 0, 0, high)
    rows = dot(picker, row_ref[...], 0, 0, high)
    rows = jnp.concatenate([rows, jnp.zeros((count, LANES - PROMPT), F32)], axis=1)
    for piece in range(pieces):
        out_ref[:, piece, :] = cols[:, piece * LANES : (piece + 1) * LANES]
    out_ref[:, pieces, :] = rows
    for piece in range(pieces + 1, out_ref.shape[1]):
        out_ref[:, piece, :] = jnp.zeros((count, LANES), F32)


def main_kernel(
    place_ref,
    pair_hbm,
    own_hbm,
    left_hbm,
    right_hbm,
    far_first_hbm,
    far_second_hbm,
    hidden_ref,
    up_ref,
    cols_ref,
    rows_ref,
    gain_ref,
    cot_ref,
    keep_ref,
    send_ref,
    unit_out,
    base_out,
    scale_out,
    line_out,
    pair,
    single,
    base,
    unit,
    normed,
    qkv,
    parts,
    scale,
    sems,
):
    width = hidden_ref.shape[1]
    tokens = hidden_ref.shape[0]
    length = PAD + tokens
    inner = up_ref.shape[1]
    depth = width // CHUNKS
    groups = cols_ref.shape[0]
    size = width // groups
    pieces = size // LANES
    member = place_ref[0]
    core = place_ref[1]

    half = single.shape[0] // 2
    copies = [
        pltpu.make_async_copy(own_hbm, single.at[:, place_ref[2]], sems.at[0]),
        pltpu.make_async_copy(left_hbm, single.at[:, place_ref[3]], sems.at[1]),
        pltpu.make_async_copy(right_hbm, single.at[:, place_ref[4]], sems.at[2]),
        pltpu.make_async_copy(far_first_hbm, single.at[:half, place_ref[5]], sems.at[3]),
        pltpu.make_async_copy(far_second_hbm, single.at[half:, place_ref[5]], sems.at[4]),
    ] + [
        pltpu.make_async_copy(
            pair_hbm.at[pl.ds(k * depth, depth), :],
            pair.at[pl.ds(k * depth, depth), :],
            sems.at[5 + k],
        )
        for k in range(CHUNKS)
    ]
    for copy in copies:
        copy.start()
    line = jnp.concatenate(
        [cols_ref[g, k : k + 1, :] for g in range(groups) for k in range(pieces)], axis=1
    )
    line_out[...] = line
    rows = as_column(rows_ref[...])
    own = pl.ds(pl.multiple_of(member * BLOCK, BLOCK), BLOCK)
    squares = jnp.zeros((PAD, 1), F32)
    for k in range(5):
        copies[k].wait()
    lead = single.shape[0] // CHUNKS
    single_part = lambda k, start, stop: single[
        k * lead : (k + 1) * lead, :, :, start:stop
    ].reshape(depth, stop - start)
    for k in range(CHUNKS):
        span = slice(k * depth, (k + 1) * depth)
        base_part = jnp.transpose(single_part(k, inner, inner + LANES).astype(F32))
        base[:, span] = base_part
        act = (base_part * rows * line[:, span]).astype(BF16).astype(F32)
        unit[:, span] = act
        squares = squares + jnp.sum(act * act, axis=1, keepdims=True)
    inverse = lax.rsqrt(squares * (1.0 / width) + norm_epsilon)
    scale[...] = jnp.where(iota((PAD, LANES), 1) == 0, inverse, rows)
    scale_own = scale[own, :]
    scale_out[...] = scale_own
    for k in range(CHUNKS):
        span = slice(k * depth, (k + 1) * depth)
        unit_part = unit[:, span] * inverse
        unit[:, span] = unit_part
        normed[:, span] = (unit_part * gain_ref[:, span]).astype(BF16)
    query_weights = single[:, :, :, :inner].reshape(width, inner)
    qkv[PAD:, :inner] = dot(hidden_ref[...], query_weights, 1, 0).astype(BF16)
    qkv[:PAD, :inner] = dot(normed[...], query_weights, 1, 0).astype(BF16)
    for k in range(CHUNKS):
        copies[5 + k].wait()
    qkv[PAD:, inner:] = dot(hidden_ref[...], pair[...], 1, 0).astype(BF16)
    qkv[:PAD, inner:] = dot(normed[...], pair[...], 1, 0).astype(BF16)

    column = iota((length, length), 1)
    real_key = (column < PROMPT) | (column >= PAD)
    along = jnp.zeros((PAD, 1), F32)
    grads = [[], [], []]
    for head in range(inner // HEAD_DIM):
        at = head * HEAD_DIM
        query = qkv[:, at : at + HEAD_DIM]
        key = qkv[:, inner + at : inner + at + HEAD_DIM]
        value = qkv[:, 2 * inner + at : 2 * inner + at + HEAD_DIM]
        up = up_ref[:, at : at + HEAD_DIM]
        exponent = jnp.where(real_key, jnp.exp(dot(query, key, 1, 1)), 0.0)
        attend = exponent / jnp.sum(exponent, axis=1, keepdims=True)
        grad_prob = dot(up, value, 1, 1)
        row_dot = jnp.sum(attend * grad_prob, axis=1, keepdims=True)
        grad_score = (attend * (grad_prob - row_dot)).astype(BF16)
        found = (
            dot(grad_score[:PAD, :], key, 1, 0).astype(BF16),
            dot(grad_score[:, :PAD], query, 0, 0).astype(BF16),
            dot(attend[:, :PAD].astype(BF16), up, 0, 0).astype(BF16),
        )
        for kind, (grad, low) in enumerate(zip(found, (query, key, value))):
            grads[kind].append(grad)
            along = along + jnp.sum(
                grad.astype(F32) * low[:PAD].astype(F32), axis=1, keepdims=True
            )
    grad_all = jnp.concatenate(grads[0] + grads[1] + grads[2], axis=1)

    mean = along * (1.0 / width)
    strength = inverse * rows
    for g in range(groups):
        span = slice(g * size, (g + 1) * size)
        place = slice(g * single.shape[0] // groups, (g + 1) * single.shape[0] // groups)
        part = dot(grad_all[:, :inner], single[place, :, :, :inner].reshape(size, inner), 1, 1)
        part = part + dot(grad_all[:, inner:], pair[span, :], 1, 1)
        parts[:, span] = part
        weighted = base[:, span] * strength
        base_own = base[own, span]
        base_out[:, span] = base_own
        unit_out[:, span] = unit[own, span]
        cols = (
            gain_ref[:, span] * jnp.sum(part * weighted, axis=0, keepdims=True)
            - jnp.sum(weighted * unit[:, span] * mean, axis=0, keepdims=True)
            + jnp.sum(
                cot_ref[:, span].astype(F32) * base_own * scale_own[:, 1:2], axis=0, keepdims=True
            )
        )
        parts[g * BLOCK : (g + 1) * BLOCK, width:] = jnp.concatenate(
            [cols[:, at : at + LANES] for at in range(0, size, LANES)]
            + [jnp.zeros((BLOCK - pieces, LANES), F32)],
            axis=0,
        )
    for pair in range(groups // 2):
        start = pl.multiple_of((2 * pair + core) * BLOCK, BLOCK)
        keep_ref[pair, :, :] = parts[pl.ds(start, BLOCK), :]
        start = pl.multiple_of((2 * pair + 1 - core) * BLOCK, BLOCK)
        send_ref[pair, :, :] = parts[pl.ds(start, BLOCK), :]


def main_part(place, pair, singles, hidden, up, cols, rows, gain, cot):
    width = hidden.shape[1]
    length = PAD + hidden.shape[0]
    inner = up.shape[1]
    ring = width // (singles[0].shape[0] * singles[0].shape[1])
    groups = cols.shape[0]
    half = jax.ShapeDtypeStruct((groups // 2, BLOCK, width + LANES), F32)
    own = jax.ShapeDtypeStruct((BLOCK, width), F32)
    return pl.pallas_call(
        main_kernel,
        out_shape=(
            half,
            half,
            own,
            own,
            jax.ShapeDtypeStruct((BLOCK, LANES), F32),
            jax.ShapeDtypeStruct((1, width), F32),
        ),
        in_specs=[SMEM, pl.BlockSpec(memory_space=pltpu.HBM)]
        + [pl.BlockSpec(memory_space=pl.ANY)] * 5
        + [VMEM] * 6,
        out_specs=(VMEM,) * 6,
        scratch_shapes=[
            pltpu.VMEM(pair.shape, BF16),
            pltpu.VMEM((singles[0].shape[0], ring) + singles[0].shape[1:], BF16),
            pltpu.VMEM((PAD, width), F32),
            pltpu.VMEM((PAD, width), F32),
            pltpu.VMEM((PAD, width), BF16),
            pltpu.VMEM((length, 3 * inner), BF16),
            pltpu.VMEM((PAD, width + LANES), F32),
            pltpu.VMEM((PAD, LANES), F32),
            pltpu.SemaphoreType.DMA((5 + CHUNKS,)),
        ],
        compiler_params=MAIN_PARAMS,
    )(place, pair, *singles, hidden, up, cols, rows, gain, cot)


def prompt_kernel(pieces, got_ref, unit_ref, base_ref, cot_ref, gain_ref, cols_ref, scale_ref, out_ref):
    width = unit_ref.shape[1]
    total = got_ref[0, :, :].astype(F32)
    for source in range(1, got_ref.shape[0]):
        total = total + got_ref[source, :, :].astype(F32)
    inverse = scale_ref[:, 0:1]
    rows = scale_ref[:, 1:2]
    unit = unit_ref[...]
    scaled = total[:, :width] * gain_ref[...]
    mean = jnp.sum(scaled * unit, axis=1, keepdims=True) * (1.0 / width)
    grad = cot_ref[...].astype(F32) + inverse * (scaled - unit * mean)
    times_cols = grad * cols_ref[...]
    grad_rows = jnp.sum(times_cols * base_ref[...], axis=1, keepdims=True)
    grad_base = times_cols * rows
    cols = total[:pieces, width:]
    spare = BLOCK - 2 * pieces
    line = jnp.sum(
        jnp.where(iota((BLOCK, LANES), 1) == iota((BLOCK, LANES), 0) + HALF, grad_rows, 0.0),
        axis=0,
        keepdims=True,
    )
    under = jnp.where(iota((spare, LANES), 0) == 0, line, 0.0)
    tail = jnp.concatenate([cols, swap_halves(cols), under], axis=0)
    first_half = iota((BLOCK, LANES), 1) < HALF
    for pair in range(width // LANES):
        block = grad_base[:, pair * LANES : (pair + 1) * LANES]
        out_ref[2 * pair, :, :] = jnp.where(first_half, block, tail).astype(BF16)
        out_ref[2 * pair + 1, :, :] = jnp.where(first_half, swap_halves(block), tail).astype(BF16)


def owner_kernel(first_ref, slot_ref, back_ref, shared_ref, col_ref):
    owned, width = col_ref.shape
    count = slot_ref.shape[1]
    pieces = width // LANES
    picker = (slot_ref[...] - first_ref[0] == iota((owned, count), 0)).astype(BF16)
    back = back_ref[...].astype(F32)
    total = jnp.sum(back, axis=0)
    first_half = iota((owned, LANES), 1) < HALF
    for piece in range(pieces):
        upper = dot(picker, back[:, piece, :].astype(BF16), 1, 0)
        lower = dot(picker, back[:, pieces + piece, :].astype(BF16), 1, 0)
        col_ref[:, piece * LANES : (piece + 1) * LANES] = jnp.where(
            first_half, swap_halves(lower), upper
        )
    rows = dot(back[:, 2 * pieces, :].astype(BF16), picker, 0, 1)
    shared = jnp.concatenate([total[:, :HALF], rows[HALF : HALF + BLOCK, :]], axis=1)
    shared_ref[...] = jnp.broadcast_to(shared[None], shared_ref.shape)


def update_kernel(grads_ref, *refs):
    grads = jnp.transpose(grads_ref[...])
    for kind in range(2):
        param, one, two, param_out, one_out, two_out = refs[kind::2]
        rows = param.shape[0]
        found = grads[kind * HALF : kind * HALF + rows, : param.shape[1]]
        param_out[...], one_out[...], two_out[...] = adam_step(param[...], one[...], two[...], found)


def local(
    hidden_rows,
    norm_gain,
    w_query,
    w_key,
    w_value,
    head_cotangent,
    prompt_cotangent,
    prompt_master,
    prompt_first,
    prompt_second,
    row_factor,
    row_first,
    row_second,
    col_factor,
    col_first,
    col_second,
    row_tenant,
    tenant_slot,
):
    dp, mp = ROWS_AXES, HEADS_AXES
    count = lax.axis_size(dp)
    groups = lax.axis_size(mp)
    device = lax.axis_index(dp)
    member = lax.axis_index(mp)
    owned, col_width = col_factor.shape
    width = hidden_rows.shape[2]
    pieces = col_width // LANES

    depth = w_query.shape[0]
    inner = w_query.shape[1]
    ring = lax.axis_size("y")
    pair = pl.pallas_call(
        lambda *refs: lead_kernel(owned, *refs),
        out_shape=jax.ShapeDtypeStruct((depth, 2 * inner + LANES), BF16),
        in_specs=[SMEM, SMEM, VMEM, VMEM],
        out_specs=VMEM,
        compiler_params=PARAMS,
    )(row_tenant, tenant_slot, w_key, w_value)
    pair = lax.all_gather(pair, "y", axis=0, tiled=True)
    marks = pair.reshape(ring, depth, -1)[:, 0, 2 * inner : 2 * inner + 2].reshape(-1)
    pair = pair[:, : 2 * inner]

    marks = jnp.broadcast_to(
        jnp.pad(marks, (0, LANES - PROMPT - marks.shape[0]))[None], (depth, LANES - PROMPT)
    )
    own = jnp.concatenate([w_query, prompt_master.T.astype(BF16), marks], axis=1)
    pair, own = lax.optimization_barrier((pair, own))
    pair = lax.all_gather(pair, "z", axis=0, tiled=True)
    own = lax.all_gather(own, "z", axis=0, tiled=False)
    half = own.shape[0] // 2
    up_ring = [(i, (i + 1) % ring) for i in range(ring)]
    down_ring = [(i, (i - 1) % ring) for i in range(ring)]
    left = lax.ppermute(own, "y", up_ring)
    right = lax.ppermute(own, "y", down_ring)
    far_first = lax.ppermute(left[:half], "y", up_ring)
    far_second = lax.ppermute(right[half:], "y", down_ring)
    singles = (own, left, right, far_first, far_second)

    marks = own[:, 0, inner + PROMPT : inner + PROMPT + 2 * ring].reshape(count, 2)
    marks = marks.astype(jnp.int32)
    slots = (marks[:, 0] * owned + marks[:, 1])[None, :]
    first = (device * owned).astype(jnp.int32).reshape(1)
    terms = pl.pallas_call(
        factor_kernel,
        out_shape=jax.ShapeDtypeStruct((count, 8, LANES), F32),
        in_specs=[SMEM, VMEM, VMEM, VMEM],
        out_specs=VMEM,
        compiler_params=PARAMS,
    )(first, slots, row_factor, col_factor)
    terms = jnp.sum(lax.all_to_all(terms, dp, 0, 0, tiled=False), axis=0)
    factor_cols = lax.all_to_all(
        jnp.broadcast_to(terms[None], (groups, 8, LANES)), mp, 0, 0, tiled=False
    )
    factor_rows = terms[pieces : pieces + 1]

    gain = norm_gain[None, :]
    hidden = hidden_rows[0].astype(F32)
    inverse = lax.rsqrt(jnp.mean(hidden * hidden, axis=-1, keepdims=True) + norm_epsilon)
    hidden = (hidden * inverse * gain).astype(BF16)
    upstream = jnp.concatenate(
        [
            jnp.pad(head_cotangent[0, :PROMPT], ((0, PAD - PROMPT), (0, 0))),
            head_cotangent[0, PROMPT:],
        ],
        axis=0,
    )
    cot = lax.dynamic_slice_in_dim(
        jnp.pad(prompt_cotangent[0], ((0, PAD - PROMPT), (0, 0))), member * BLOCK, BLOCK, 0
    )
    y = lax.axis_index("y")
    place = jnp.stack(
        [member, lax.axis_index("c"), y, (y - 1) % ring, (y + 1) % ring, (y + 2) % ring]
    ).astype(jnp.int32)
    keep, send, unit_own, base_own, scale_own, line = main_part(
        place, pair, singles, hidden, upstream, factor_cols, factor_rows, gain, cot
    )

    parts = (keep + lax.ppermute(send, "c", [(0, 1), (1, 0)])).astype(BF16)
    parts = lax.all_to_all(parts, "x", 0, 0, tiled=False)
    outgoing = pl.pallas_call(
        lambda *refs: prompt_kernel(pieces, *refs),
        out_shape=jax.ShapeDtypeStruct((count, BLOCK, LANES), BF16),
        in_specs=[VMEM] * 7,
        out_specs=VMEM,
        compiler_params=PARAMS,
    )(parts, unit_own, base_own, cot, gain, line, scale_own)

    back = lax.all_to_all(outgoing, dp, 0, 0, tiled=False)
    shared, col_grad = pl.pallas_call(
        owner_kernel,
        out_shape=(
            jax.ShapeDtypeStruct((groups, BLOCK, LANES), F32),
            jax.ShapeDtypeStruct((owned, col_width), F32),
        ),
        in_specs=[SMEM, VMEM, VMEM],
        out_specs=(VMEM, VMEM),
        compiler_params=PARAMS,
    )(first, slots, back)
    shared = lax.all_to_all(shared, mp, 0, 0, tiled=False).reshape(PAD, LANES)
    operands = [
        part
        for pair in zip(
            (prompt_master.T, prompt_first.T, prompt_second.T), (row_factor, row_first, row_second)
        )
        for part in pair
    ]
    new = pl.pallas_call(
        update_kernel,
        out_shape=tuple(jax.ShapeDtypeStruct(part.shape, F32) for part in operands),
        in_specs=[VMEM] * 7,
        out_specs=(VMEM,) * 6,
        compiler_params=PARAMS,
    )(shared, *operands)
    return (
        *(part.T for part in new[0::2]),
        *new[1::2],
        *adam_step(col_factor, col_first, col_second, col_grad),
    )


def solution(mesh):
    ring = 4 if mesh.shape["dp"] % 4 == 0 else 2
    devices = mesh.devices.reshape(mesh.shape["dp"] // ring, ring, mesh.shape["mp"] // 2, 2)
    dp, mp = ROWS_AXES, HEADS_AXES
    return jax.shard_map(
        local,
        mesh=Mesh(devices, dp + mp),
        in_specs=(
            P(dp, None, None),
            P(),
            P(dp, mp),
            P(dp, mp),
            P(dp, mp),
            P(dp, None, mp),
            P(dp, None, None),
            P(None, dp),
            P(None, dp),
            P(None, dp),
            P(dp, None),
            P(dp, None),
            P(dp, None),
            P(dp, mp),
            P(dp, mp),
            P(dp, mp),
            P(dp),
            P(),
        ),
        out_specs=(
            P(None, dp),
            P(None, dp),
            P(None, dp),
            P(dp, None),
            P(dp, None),
            P(dp, None),
            P(dp, mp),
            P(dp, mp),
            P(dp, mp),
        ),
        check_vma=False,
    )
```

```python
import jax
import jax.numpy as jnp
from jax import lax
from jax.experimental import pallas as pl
from jax.experimental.pallas import tpu as pltpu
from jax.sharding import Mesh, PartitionSpec as P

HEAD_DIM = 64
PROMPT = 100
PAD = 128
BLOCK = 16
LANES = 128
HALF = 64
CHUNKS = 4

beta_first = 0.9
beta_second = 0.99
learn_rate = 0.01
adam_epsilon = 1e-08
norm_epsilon = 1e-06

ROWS_AXES = ("z", "y")
HEADS_AXES = ("x", "c")
BF16 = jnp.bfloat16
F32 = jnp.float32
VMEM = pl.BlockSpec(memory_space=pltpu.VMEM)
SMEM = pl.BlockSpec(memory_space=pltpu.SMEM)
PARAMS = pltpu.CompilerParams(vmem_limit_bytes=16 * 1024 * 1024)
MAIN_PARAMS = pltpu.CompilerParams(vmem_limit_bytes=50 * 1024 * 1024)
ALONE_PARAMS = pltpu.CompilerParams(vmem_limit_bytes=58 * 1024 * 1024)


def adam_step(param, moment_one, moment_two, gradient):
    first_new = beta_first * moment_one + (1.0 - beta_first) * gradient
    second_new = beta_second * moment_two + (1.0 - beta_second) * gradient * gradient
    return (
        param - learn_rate * first_new / (jnp.sqrt(second_new) + adam_epsilon),
        first_new,
        second_new,
    )


def dot(a, b, da, db, precision=None):
    return lax.dot_general(
        a, b, (((da,), (db,)), ((), ())), preferred_element_type=F32, precision=precision
    )


def iota(shape, axis):
    return lax.broadcasted_iota(jnp.int32, shape, axis)


def swap_halves(array):
    return jnp.concatenate([array[:, HALF:], array[:, :HALF]], axis=1)


def as_column(line):
    size = line.shape[1]
    eye = iota((size, size), 0) == iota((size, size), 1)
    return jnp.sum(jnp.where(eye, line, 0.0), axis=1, keepdims=True)


def lead_kernel(owned, tenant_ref, slot_ref, key_ref, value_ref, out_ref):
    depth, inner = key_ref.shape
    slot = slot_ref[tenant_ref[0]]
    owner = lax.div(slot, owned)
    lane = iota((depth, LANES), 1)
    marks = jnp.where(lane == 0, owner, jnp.where(lane == 1, slot - owner * owned, 0))
    out_ref[:, :inner] = key_ref[...]
    out_ref[:, inner : 2 * inner] = value_ref[...]
    out_ref[:, 2 * inner :] = marks.astype(F32).astype(BF16)


def factor_kernel(first_ref, slot_ref, row_ref, col_ref, out_ref):
    owned, width = col_ref.shape
    count = slot_ref.shape[1]
    pieces = width // LANES
    picker = (slot_ref[...] - first_ref[0] == iota((owned, count), 0)).astype(F32)
    high = lax.Precision.HIGHEST
    cols = dot(picker, col_ref[...], 0, 0, high)
    rows = dot(picker, row_ref[...], 0, 0, high)
    rows = jnp.concatenate([rows, jnp.zeros((count, LANES - PROMPT), F32)], axis=1)
    for piece in range(pieces):
        out_ref[:, piece, :] = cols[:, piece * LANES : (piece + 1) * LANES]
    out_ref[:, pieces, :] = rows
    for piece in range(pieces + 1, out_ref.shape[1]):
        out_ref[:, piece, :] = jnp.zeros((count, LANES), F32)


def main_kernel(
    place_ref,
    pair_hbm,
    own_hbm,
    left_hbm,
    right_hbm,
    far_first_hbm,
    far_second_hbm,
    hidden_ref,
    up_ref,
    cols_ref,
    rows_ref,
    gain_ref,
    cot_ref,
    keep_ref,
    send_ref,
    unit_out,
    base_out,
    scale_out,
    line_out,
    pair,
    single,
    base,
    unit,
    normed,
    qkv,
    parts,
    scale,
    sems,
):
    width = hidden_ref.shape[1]
    tokens = hidden_ref.shape[0]
    length = PAD + tokens
    inner = up_ref.shape[1]
    depth = width // CHUNKS
    groups = cols_ref.shape[0]
    size = width // groups
    pieces = size // LANES
    member = place_ref[0]
    core = place_ref[1]

    half = single.shape[0] // 2
    copies = [
        pltpu.make_async_copy(own_hbm, single.at[:, place_ref[2]], sems.at[0]),
        pltpu.make_async_copy(left_hbm, single.at[:, place_ref[3]], sems.at[1]),
        pltpu.make_async_copy(right_hbm, single.at[:, place_ref[4]], sems.at[2]),
        pltpu.make_async_copy(far_first_hbm, single.at[:half, place_ref[5]], sems.at[3]),
        pltpu.make_async_copy(far_second_hbm, single.at[half:, place_ref[5]], sems.at[4]),
    ] + [
        pltpu.make_async_copy(
            pair_hbm.at[pl.ds(k * depth, depth), :],
            pair.at[pl.ds(k * depth, depth), :],
            sems.at[5 + k],
        )
        for k in range(CHUNKS)
    ]
    for copy in copies:
        copy.start()
    line = jnp.concatenate(
        [cols_ref[g, k : k + 1, :] for g in range(groups) for k in range(pieces)], axis=1
    )
    line_out[...] = line
    rows = as_column(rows_ref[...])
    own = pl.ds(pl.multiple_of(member * BLOCK, BLOCK), BLOCK)
    squares = jnp.zeros((PAD, 1), F32)
    for k in range(5):
        copies[k].wait()
    lead = single.shape[0] // CHUNKS
    single_part = lambda k, start, stop: single[
        k * lead : (k + 1) * lead, :, :, start:stop
    ].reshape(depth, stop - start)
    for k in range(CHUNKS):
        span = slice(k * depth, (k + 1) * depth)
        base_part = jnp.transpose(single_part(k, inner, inner + LANES).astype(F32))
        base[:, span] = base_part
        act = (base_part * rows * line[:, span]).astype(BF16).astype(F32)
        unit[:, span] = act
        squares = squares + jnp.sum(act * act, axis=1, keepdims=True)
    inverse = lax.rsqrt(squares * (1.0 / width) + norm_epsilon)
    scale[...] = jnp.where(iota((PAD, LANES), 1) == 0, inverse, rows)
    scale_own = scale[own, :]
    scale_out[...] = scale_own
    for k in range(CHUNKS):
        span = slice(k * depth, (k + 1) * depth)
        unit_part = unit[:, span] * inverse
        unit[:, span] = unit_part
        normed[:, span] = (unit_part * gain_ref[:, span]).astype(BF16)
    query_weights = single[:, :, :, :inner].reshape(width, inner)
    qkv[PAD:, :inner] = dot(hidden_ref[...], query_weights, 1, 0).astype(BF16)
    qkv[:PAD, :inner] = dot(normed[...], query_weights, 1, 0).astype(BF16)
    for k in range(CHUNKS):
        copies[5 + k].wait()
    qkv[PAD:, inner:] = dot(hidden_ref[...], pair[...], 1, 0).astype(BF16)
    qkv[:PAD, inner:] = dot(normed[...], pair[...], 1, 0).astype(BF16)

    column = iota((length, length), 1)
    real_key = (column < PROMPT) | (column >= PAD)
    along = jnp.zeros((PAD, 1), F32)
    grads = [[], [], []]
    for head in range(inner // HEAD_DIM):
        at = head * HEAD_DIM
        query = qkv[:, at : at + HEAD_DIM]
        key = qkv[:, inner + at : inner + at + HEAD_DIM]
        value = qkv[:, 2 * inner + at : 2 * inner + at + HEAD_DIM]
        up = up_ref[:, at : at + HEAD_DIM]
        exponent = jnp.where(real_key, jnp.exp(dot(query, key, 1, 1)), 0.0)
        attend = exponent / jnp.sum(exponent, axis=1, keepdims=True)
        grad_prob = dot(up, value, 1, 1)
        row_dot = jnp.sum(attend * grad_prob, axis=1, keepdims=True)
        grad_score = (attend * (grad_prob - row_dot)).astype(BF16)
        found = (
            dot(grad_score[:PAD, :], key, 1, 0).astype(BF16),
            dot(grad_score[:, :PAD], query, 0, 0).astype(BF16),
            dot(attend[:, :PAD].astype(BF16), up, 0, 0).astype(BF16),
        )
        for kind, (grad, low) in enumerate(zip(found, (query, key, value))):
            grads[kind].append(grad)
            along = along + jnp.sum(
                grad.astype(F32) * low[:PAD].astype(F32), axis=1, keepdims=True
            )
    grad_all = jnp.concatenate(grads[0] + grads[1] + grads[2], axis=1)

    mean = along * (1.0 / width)
    strength = inverse * rows
    for g in range(groups):
        span = slice(g * size, (g + 1) * size)
        place = slice(g * single.shape[0] // groups, (g + 1) * single.shape[0] // groups)
        part = dot(grad_all[:, :inner], single[place, :, :, :inner].reshape(size, inner), 1, 1)
        part = part + dot(grad_all[:, inner:], pair[span, :], 1, 1)
        parts[:, span] = part
        weighted = base[:, span] * strength
        base_own = base[own, span]
        base_out[:, span] = base_own
        unit_out[:, span] = unit[own, span]
        cols = (
            gain_ref[:, span] * jnp.sum(part * weighted, axis=0, keepdims=True)
            - jnp.sum(weighted * unit[:, span] * mean, axis=0, keepdims=True)
            + jnp.sum(
                cot_ref[:, span].astype(F32) * base_own * scale_own[:, 1:2], axis=0, keepdims=True
            )
        )
        parts[g * BLOCK : (g + 1) * BLOCK, width:] = jnp.concatenate(
            [cols[:, at : at + LANES] for at in range(0, size, LANES)]
            + [jnp.zeros((BLOCK - pieces, LANES), F32)],
            axis=0,
        )
    for pair in range(groups // 2):
        start = pl.multiple_of((2 * pair + core) * BLOCK, BLOCK)
        keep_ref[pair, :, :] = parts[pl.ds(start, BLOCK), :]
        start = pl.multiple_of((2 * pair + 1 - core) * BLOCK, BLOCK)
        send_ref[pair, :, :] = parts[pl.ds(start, BLOCK), :]


def main_part(place, pair, singles, hidden, up, cols, rows, gain, cot):
    width = hidden.shape[1]
    length = PAD + hidden.shape[0]
    inner = up.shape[1]
    ring = width // (singles[0].shape[0] * singles[0].shape[1])
    groups = cols.shape[0]
    half = jax.ShapeDtypeStruct((groups // 2, BLOCK, width + LANES), F32)
    own = jax.ShapeDtypeStruct((BLOCK, width), F32)
    return pl.pallas_call(
        main_kernel,
        out_shape=(
            half,
            half,
            own,
            own,
            jax.ShapeDtypeStruct((BLOCK, LANES), F32),
            jax.ShapeDtypeStruct((1, width), F32),
        ),
        in_specs=[SMEM, pl.BlockSpec(memory_space=pl.ANY)]
        + [pl.BlockSpec(memory_space=pl.ANY)] * 5
        + [VMEM] * 6,
        out_specs=(VMEM,) * 6,
        scratch_shapes=[
            pltpu.VMEM(pair.shape, BF16),
            pltpu.VMEM((singles[0].shape[0], ring) + singles[0].shape[1:], BF16),
            pltpu.VMEM((PAD, width), F32),
            pltpu.VMEM((PAD, width), F32),
            pltpu.VMEM((PAD, width), BF16),
            pltpu.VMEM((length, 3 * inner), BF16),
            pltpu.VMEM((PAD, width + LANES), F32),
            pltpu.VMEM((PAD, LANES), F32),
            pltpu.SemaphoreType.DMA((5 + CHUNKS,)),
        ],
        compiler_params=MAIN_PARAMS,
    )(place, pair, *singles, hidden, up, cols, rows, gain, cot)


def prompt_kernel(pieces, got_ref, unit_ref, base_ref, cot_ref, gain_ref, cols_ref, scale_ref, out_ref):
    width = unit_ref.shape[1]
    total = got_ref[0, :, :].astype(F32)
    for source in range(1, got_ref.shape[0]):
        total = total + got_ref[source, :, :].astype(F32)
    inverse = scale_ref[:, 0:1]
    rows = scale_ref[:, 1:2]
    unit = unit_ref[...]
    scaled = total[:, :width] * gain_ref[...]
    mean = jnp.sum(scaled * unit, axis=1, keepdims=True) * (1.0 / width)
    grad = cot_ref[...].astype(F32) + inverse * (scaled - unit * mean)
    times_cols = grad * cols_ref[...]
    grad_rows = jnp.sum(times_cols * base_ref[...], axis=1, keepdims=True)
    grad_base = times_cols * rows
    cols = total[:pieces, width:]
    spare = BLOCK - 2 * pieces
    line = jnp.sum(
        jnp.where(iota((BLOCK, LANES), 1) == iota((BLOCK, LANES), 0) + HALF, grad_rows, 0.0),
        axis=0,
        keepdims=True,
    )
    under = jnp.where(iota((spare, LANES), 0) == 0, line, 0.0)
    tail = jnp.concatenate([cols, swap_halves(cols), under], axis=0)
    first_half = iota((BLOCK, LANES), 1) < HALF
    for pair in range(width // LANES):
        block = grad_base[:, pair * LANES : (pair + 1) * LANES]
        out_ref[2 * pair, :, :] = jnp.where(first_half, block, tail).astype(BF16)
        out_ref[2 * pair + 1, :, :] = jnp.where(first_half, swap_halves(block), tail).astype(BF16)


def owner_kernel(first_ref, slot_ref, back_ref, shared_ref, col_ref):
    owned, width = col_ref.shape
    count = slot_ref.shape[1]
    pieces = width // LANES
    picker = (slot_ref[...] - first_ref[0] == iota((owned, count), 0)).astype(BF16)
    back = back_ref[...].astype(F32)
    total = jnp.sum(back, axis=0)
    first_half = iota((owned, LANES), 1) < HALF
    for piece in range(pieces):
        upper = dot(picker, back[:, piece, :].astype(BF16), 1, 0)
        lower = dot(picker, back[:, pieces + piece, :].astype(BF16), 1, 0)
        col_ref[:, piece * LANES : (piece + 1) * LANES] = jnp.where(
            first_half, swap_halves(lower), upper
        )
    rows = dot(back[:, 2 * pieces, :].astype(BF16), picker, 0, 1)
    shared = jnp.concatenate([total[:, :HALF], rows[HALF : HALF + BLOCK, :]], axis=1)
    shared_ref[...] = jnp.broadcast_to(shared[None], shared_ref.shape)


def update_kernel(grads_ref, *refs):
    grads = jnp.transpose(grads_ref[...])
    for kind in range(2):
        param, one, two, param_out, one_out, two_out = refs[kind::2]
        rows = param.shape[0]
        found = grads[kind * HALF : kind * HALF + rows, : param.shape[1]]
        param_out[...], one_out[...], two_out[...] = adam_step(param[...], one[...], two[...], found)


def local(
    hidden_rows,
    norm_gain,
    w_query,
    w_key,
    w_value,
    head_cotangent,
    prompt_cotangent,
    prompt_master,
    prompt_first,
    prompt_second,
    row_factor,
    row_first,
    row_second,
    col_factor,
    col_first,
    col_second,
    row_tenant,
    tenant_slot,
):
    dp, mp = ROWS_AXES, HEADS_AXES
    count = lax.axis_size(dp)
    groups = lax.axis_size(mp)
    device = lax.axis_index(dp)
    member = lax.axis_index(mp)
    owned, col_width = col_factor.shape
    width = hidden_rows.shape[2]
    pieces = col_width // LANES

    depth = w_query.shape[0]
    inner = w_query.shape[1]
    ring = lax.axis_size("y")
    pair = pl.pallas_call(
        lambda *refs: lead_kernel(owned, *refs),
        out_shape=jax.ShapeDtypeStruct((depth, 2 * inner + LANES), BF16),
        in_specs=[SMEM, SMEM, VMEM, VMEM],
        out_specs=VMEM,
        compiler_params=ALONE_PARAMS,
    )(row_tenant, tenant_slot, w_key, w_value)
    pair = lax.all_gather(pair, "y", axis=0, tiled=True)
    marks = pair.reshape(ring, depth, -1)[:, 0, 2 * inner : 2 * inner + 2].reshape(-1)
    pair = pair[:, : 2 * inner]

    marks = jnp.broadcast_to(
        jnp.pad(marks, (0, LANES - PROMPT - marks.shape[0]))[None], (depth, LANES - PROMPT)
    )
    own = jnp.concatenate([w_query, prompt_master.T.astype(BF16), marks], axis=1)
    pair, own = lax.optimization_barrier((pair, own))
    pair = lax.all_gather(pair, "z", axis=0, tiled=True)
    own = lax.all_gather(own, "z", axis=0, tiled=False)
    half = own.shape[0] // 2
    up_ring = [(i, (i + 1) % ring) for i in range(ring)]
    down_ring = [(i, (i - 1) % ring) for i in range(ring)]
    left = lax.ppermute(own, "y", up_ring)
    right = lax.ppermute(own, "y", down_ring)
    far_first = lax.ppermute(left[:half], "y", up_ring)
    far_second = lax.ppermute(right[half:], "y", down_ring)
    singles = (own, left, right, far_first, far_second)

    marks = own[:, 0, inner + PROMPT : inner + PROMPT + 2 * ring].reshape(count, 2)
    marks = marks.astype(jnp.int32)
    slots = (marks[:, 0] * owned + marks[:, 1])[None, :]
    first = (device * owned).astype(jnp.int32).reshape(1)
    terms = pl.pallas_call(
        factor_kernel,
        out_shape=jax.ShapeDtypeStruct((count, 8, LANES), F32),
        in_specs=[SMEM, VMEM, VMEM, VMEM],
        out_specs=VMEM,
        compiler_params=ALONE_PARAMS,
    )(first, slots, row_factor, col_factor)
    terms = jnp.sum(lax.all_to_all(terms, dp, 0, 0, tiled=False), axis=0)
    factor_cols = lax.all_to_all(
        jnp.broadcast_to(terms[None], (groups, 8, LANES)), mp, 0, 0, tiled=False
    )
    factor_rows = terms[pieces : pieces + 1]

    gain = norm_gain[None, :]
    hidden = hidden_rows[0].astype(F32)
    inverse = lax.rsqrt(jnp.mean(hidden * hidden, axis=-1, keepdims=True) + norm_epsilon)
    hidden = (hidden * inverse * gain).astype(BF16)
    upstream = jnp.concatenate(
        [
            jnp.pad(head_cotangent[0, :PROMPT], ((0, PAD - PROMPT), (0, 0))),
            head_cotangent[0, PROMPT:],
        ],
        axis=0,
    )
    cot = lax.dynamic_slice_in_dim(
        jnp.pad(prompt_cotangent[0], ((0, PAD - PROMPT), (0, 0))), member * BLOCK, BLOCK, 0
    )
    y = lax.axis_index("y")
    place = jnp.stack(
        [member, lax.axis_index("c"), y, (y - 1) % ring, (y + 1) % ring, (y + 2) % ring]
    ).astype(jnp.int32)
    keep, send, unit_own, base_own, scale_own, line = main_part(
        place, pair, singles, hidden, upstream, factor_cols, factor_rows, gain, cot
    )

    parts = (keep + lax.ppermute(send, "c", [(0, 1), (1, 0)])).astype(BF16)
    parts = lax.all_to_all(parts, "x", 0, 0, tiled=False)
    outgoing = pl.pallas_call(
        lambda *refs: prompt_kernel(pieces, *refs),
        out_shape=jax.ShapeDtypeStruct((count, BLOCK, LANES), BF16),
        in_specs=[VMEM] * 7,
        out_specs=VMEM,
        compiler_params=PARAMS,
    )(parts, unit_own, base_own, cot, gain, line, scale_own)

    back = lax.all_to_all(outgoing, dp, 0, 0, tiled=False)
    shared, col_grad = pl.pallas_call(
        owner_kernel,
        out_shape=(
            jax.ShapeDtypeStruct((groups, BLOCK, LANES), F32),
            jax.ShapeDtypeStruct((owned, col_width), F32),
        ),
        in_specs=[SMEM, VMEM, VMEM],
        out_specs=(VMEM, VMEM),
        compiler_params=PARAMS,
    )(first, slots, back)
    shared = lax.all_to_all(shared, mp, 0, 0, tiled=False).reshape(PAD, LANES)
    operands = [
        part
        for pair in zip(
            (prompt_master.T, prompt_first.T, prompt_second.T), (row_factor, row_first, row_second)
        )
        for part in pair
    ]
    new = pl.pallas_call(
        update_kernel,
        out_shape=tuple(jax.ShapeDtypeStruct(part.shape, F32) for part in operands),
        in_specs=[VMEM] * 7,
        out_specs=(VMEM,) * 6,
        compiler_params=PARAMS,
    )(shared, *operands)
    return (
        *(part.T for part in new[0::2]),
        *new[1::2],
        *adam_step(col_factor, col_first, col_second, col_grad),
    )


def solution(mesh):
    ring = 4 if mesh.shape["dp"] % 4 == 0 else 2
    devices = mesh.devices.reshape(mesh.shape["dp"] // ring, ring, mesh.shape["mp"] // 2, 2)
    dp, mp = ROWS_AXES, HEADS_AXES
    return jax.shard_map(
        local,
        mesh=Mesh(devices, dp + mp),
        in_specs=(
            P(dp, None, None),
            P(),
            P(dp, mp),
            P(dp, mp),
            P(dp, mp),
            P(dp, None, mp),
            P(dp, None, None),
            P(None, dp),
            P(None, dp),
            P(None, dp),
            P(dp, None),
            P(dp, None),
            P(dp, None),
            P(dp, mp),
            P(dp, mp),
            P(dp, mp),
            P(dp),
            P(),
        ),
        out_specs=(
            P(None, dp),
            P(None, dp),
            P(None, dp),
            P(dp, None),
            P(dp, None),
            P(dp, None),
            P(dp, mp),
            P(dp, mp),
            P(dp, mp),
        ),
        check_vma=False,
    )
```

```python
import jax
import jax.numpy as jnp
from jax import lax
from jax.experimental import pallas as pl
from jax.experimental.pallas import tpu as pltpu
from jax.sharding import Mesh, PartitionSpec as P

HEAD_DIM = 64
PROMPT = 100
PAD = 128
BLOCK = 16
LANES = 128
HALF = 64
CHUNKS = 4

beta_first = 0.9
beta_second = 0.99
learn_rate = 0.01
adam_epsilon = 1e-08
norm_epsilon = 1e-06

ROWS_AXES = ("z", "y")
HEADS_AXES = ("x", "c")
BF16 = jnp.bfloat16
F32 = jnp.float32
VMEM = pl.BlockSpec(memory_space=pltpu.VMEM)
SMEM = pl.BlockSpec(memory_space=pltpu.SMEM)
PARAMS = pltpu.CompilerParams(vmem_limit_bytes=16 * 1024 * 1024)
MAIN_PARAMS = pltpu.CompilerParams(vmem_limit_bytes=50 * 1024 * 1024)
ALONE_PARAMS = pltpu.CompilerParams(vmem_limit_bytes=58 * 1024 * 1024)


def adam_step(param, moment_one, moment_two, gradient):
    first_new = beta_first * moment_one + (1.0 - beta_first) * gradient
    second_new = beta_second * moment_two + (1.0 - beta_second) * gradient * gradient
    return (
        param - learn_rate * first_new / (jnp.sqrt(second_new) + adam_epsilon),
        first_new,
        second_new,
    )


def dot(a, b, da, db, precision=None):
    return lax.dot_general(
        a, b, (((da,), (db,)), ((), ())), preferred_element_type=F32, precision=precision
    )


def iota(shape, axis):
    return lax.broadcasted_iota(jnp.int32, shape, axis)


def swap_halves(array):
    return jnp.concatenate([array[:, HALF:], array[:, :HALF]], axis=1)


def as_column(line):
    size = line.shape[1]
    eye = iota((size, size), 0) == iota((size, size), 1)
    return jnp.sum(jnp.where(eye, line, 0.0), axis=1, keepdims=True)


def lead_kernel(owned, tenant_ref, slot_ref, key_ref, value_ref, out_ref):
    depth, inner = key_ref.shape
    slot = slot_ref[tenant_ref[0]]
    owner = lax.div(slot, owned)
    lane = iota((depth, LANES), 1)
    marks = jnp.where(lane == 0, owner, jnp.where(lane == 1, slot - owner * owned, 0))
    out_ref[:, :inner] = key_ref[...]
    out_ref[:, inner : 2 * inner] = value_ref[...]
    out_ref[:, 2 * inner :] = marks.astype(F32).astype(BF16)


def factor_kernel(first_ref, slot_ref, row_ref, col_ref, out_ref):
    owned, width = col_ref.shape
    count = slot_ref.shape[1]
    pieces = width // LANES
    picker = (slot_ref[...] - first_ref[0] == iota((owned, count), 0)).astype(F32)
    high = lax.Precision.HIGHEST
    cols = dot(picker, col_ref[...], 0, 0, high)
    rows = dot(picker, row_ref[...], 0, 0, high)
    rows = jnp.concatenate([rows, jnp.zeros((count, LANES - PROMPT), F32)], axis=1)
    for piece in range(pieces):
        out_ref[:, piece, :] = cols[:, piece * LANES : (piece + 1) * LANES]
    out_ref[:, pieces, :] = rows
    for piece in range(pieces + 1, out_ref.shape[1]):
        out_ref[:, piece, :] = jnp.zeros((count, LANES), F32)


def main_kernel(
    place_ref,
    pair_hbm,
    own_hbm,
    left_hbm,
    right_hbm,
    far_first_hbm,
    far_second_hbm,
    hidden_ref,
    up_ref,
    cols_ref,
    rows_ref,
    gain_ref,
    cot_ref,
    keep_ref,
    send_ref,
    unit_out,
    base_out,
    scale_out,
    line_out,
    pair,
    single,
    base,
    unit,
    normed,
    qkv,
    parts,
    scale,
    sems,
):
    width = hidden_ref.shape[1]
    tokens = hidden_ref.shape[0]
    length = PAD + tokens
    inner = up_ref.shape[1]
    depth = width // CHUNKS
    groups = cols_ref.shape[0]
    size = width // groups
    pieces = size // LANES
    member = place_ref[0]
    core = place_ref[1]

    half = single.shape[0] // 2
    copies = [
        pltpu.make_async_copy(own_hbm, single.at[:, place_ref[2]], sems.at[0]),
        pltpu.make_async_copy(left_hbm, single.at[:, place_ref[3]], sems.at[1]),
        pltpu.make_async_copy(right_hbm, single.at[:, place_ref[4]], sems.at[2]),
        pltpu.make_async_copy(far_first_hbm, single.at[:half, place_ref[5]], sems.at[3]),
        pltpu.make_async_copy(far_second_hbm, single.at[half:, place_ref[5]], sems.at[4]),
    ] + [
        pltpu.make_async_copy(
            pair_hbm.at[pl.ds(k * depth, depth), :],
            pair.at[pl.ds(k * depth, depth), :],
            sems.at[5 + k],
        )
        for k in range(CHUNKS)
    ]
    for copy in copies:
        copy.start()
    line = jnp.concatenate(
        [cols_ref[g, k : k + 1, :] for g in range(groups) for k in range(pieces)], axis=1
    )
    line_out[...] = line
    rows = as_column(rows_ref[...])
    own = pl.ds(pl.multiple_of(member * BLOCK, BLOCK), BLOCK)
    squares = jnp.zeros((PAD, 1), F32)
    for k in range(5):
        copies[k].wait()
    lead = single.shape[0] // CHUNKS
    single_part = lambda k, start, stop: single[
        k * lead : (k + 1) * lead, :, :, start:stop
    ].reshape(depth, stop - start)
    for k in range(CHUNKS):
        span = slice(k * depth, (k + 1) * depth)
        base_part = jnp.transpose(single_part(k, inner, inner + LANES).astype(F32))
        base[:, span] = base_part
        act = (base_part * rows * line[:, span]).astype(BF16).astype(F32)
        unit[:, span] = act
        squares = squares + jnp.sum(act * act, axis=1, keepdims=True)
    inverse = lax.rsqrt(squares * (1.0 / width) + norm_epsilon)
    scale[...] = jnp.where(iota((PAD, LANES), 1) == 0, inverse, rows)
    scale_own = scale[own, :]
    scale_out[...] = scale_own
    for k in range(CHUNKS):
        span = slice(k * depth, (k + 1) * depth)
        unit_part = unit[:, span] * inverse
        unit[:, span] = unit_part
        normed[:, span] = (unit_part * gain_ref[:, span]).astype(BF16)
    query_weights = single[:, :, :, :inner].reshape(width, inner)
    qkv[PAD:, :inner] = dot(hidden_ref[...], query_weights, 1, 0).astype(BF16)
    qkv[:PAD, :inner] = dot(normed[...], query_weights, 1, 0).astype(BF16)
    for k in range(CHUNKS):
        copies[5 + k].wait()
    qkv[PAD:, inner:] = dot(hidden_ref[...], pair[...], 1, 0).astype(BF16)
    qkv[:PAD, inner:] = dot(normed[...], pair[...], 1, 0).astype(BF16)

    column = iota((length, length), 1)
    real_key = (column < PROMPT) | (column >= PAD)
    along = jnp.zeros((PAD, 1), F32)
    grads = [[], [], []]
    for head in range(inner // HEAD_DIM):
        at = head * HEAD_DIM
        query = qkv[:, at : at + HEAD_DIM]
        key = qkv[:, inner + at : inner + at + HEAD_DIM]
        value = qkv[:, 2 * inner + at : 2 * inner + at + HEAD_DIM]
        up = up_ref[:, at : at + HEAD_DIM]
        exponent = jnp.where(real_key, jnp.exp(dot(query, key, 1, 1)), 0.0)
        attend = exponent / jnp.sum(exponent, axis=1, keepdims=True)
        grad_prob = dot(up, value, 1, 1)
        row_dot = jnp.sum(attend * grad_prob, axis=1, keepdims=True)
        grad_score = (attend * (grad_prob - row_dot)).astype(BF16)
        found = (
            dot(grad_score[:PAD, :], key, 1, 0).astype(BF16),
            dot(grad_score[:, :PAD], query, 0, 0).astype(BF16),
            dot(attend[:, :PAD].astype(BF16), up, 0, 0).astype(BF16),
        )
        for kind, (grad, low) in enumerate(zip(found, (query, key, value))):
            grads[kind].append(grad)
            along = along + jnp.sum(
                grad.astype(F32) * low[:PAD].astype(F32), axis=1, keepdims=True
            )
    grad_all = jnp.concatenate(grads[0] + grads[1] + grads[2], axis=1)

    mean = along * (1.0 / width)
    strength = inverse * rows
    for g in range(groups):
        span = slice(g * size, (g + 1) * size)
        place = slice(g * single.shape[0] // groups, (g + 1) * single.shape[0] // groups)
        part = dot(grad_all[:, :inner], single[place, :, :, :inner].reshape(size, inner), 1, 1)
        part = part + dot(grad_all[:, inner:], pair[span, :], 1, 1)
        parts[:, span] = part
        weighted = base[:, span] * strength
        base_own = base[own, span]
        base_out[:, span] = base_own
        unit_out[:, span] = unit[own, span]
        cols = (
            gain_ref[:, span] * jnp.sum(part * weighted, axis=0, keepdims=True)
            - jnp.sum(weighted * unit[:, span] * mean, axis=0, keepdims=True)
            + jnp.sum(
                cot_ref[:, span].astype(F32) * base_own * scale_own[:, 1:2], axis=0, keepdims=True
            )
        )
        parts[g * BLOCK : (g + 1) * BLOCK, width:] = jnp.concatenate(
            [cols[:, at : at + LANES] for at in range(0, size, LANES)]
            + [jnp.zeros((BLOCK - pieces, LANES), F32)],
            axis=0,
        )
    for pair in range(groups // 2):
        start = pl.multiple_of((2 * pair + core) * BLOCK, BLOCK)
        keep_ref[pair, :, :] = parts[pl.ds(start, BLOCK), :]
        start = pl.multiple_of((2 * pair + 1 - core) * BLOCK, BLOCK)
        send_ref[pair, :, :] = parts[pl.ds(start, BLOCK), :].astype(BF16)


def main_part(place, pair, singles, hidden, up, cols, rows, gain, cot):
    width = hidden.shape[1]
    length = PAD + hidden.shape[0]
    inner = up.shape[1]
    ring = width // (singles[0].shape[0] * singles[0].shape[1])
    groups = cols.shape[0]
    half = (groups // 2, BLOCK, width + LANES)
    own = jax.ShapeDtypeStruct((BLOCK, width), F32)
    return pl.pallas_call(
        main_kernel,
        out_shape=(
            jax.ShapeDtypeStruct(half, F32),
            jax.ShapeDtypeStruct(half, BF16),
            own,
            own,
            jax.ShapeDtypeStruct((BLOCK, LANES), F32),
            jax.ShapeDtypeStruct((1, width), F32),
        ),
        in_specs=[SMEM, pl.BlockSpec(memory_space=pl.ANY)]
        + [pl.BlockSpec(memory_space=pl.ANY)] * 5
        + [VMEM] * 6,
        out_specs=(VMEM,) * 6,
        scratch_shapes=[
            pltpu.VMEM(pair.shape, BF16),
            pltpu.VMEM((singles[0].shape[0], ring) + singles[0].shape[1:], BF16),
            pltpu.VMEM((PAD, width), F32),
            pltpu.VMEM((PAD, width), F32),
            pltpu.VMEM((PAD, width), BF16),
            pltpu.VMEM((length, 3 * inner), BF16),
            pltpu.VMEM((PAD, width + LANES), F32),
            pltpu.VMEM((PAD, LANES), F32),
            pltpu.SemaphoreType.DMA((5 + CHUNKS,)),
        ],
        compiler_params=MAIN_PARAMS,
    )(place, pair, *singles, hidden, up, cols, rows, gain, cot)


def prompt_kernel(pieces, got_ref, unit_ref, base_ref, cot_ref, gain_ref, cols_ref, scale_ref, out_ref):
    width = unit_ref.shape[1]
    total = got_ref[0, :, :].astype(F32)
    for source in range(1, got_ref.shape[0]):
        total = total + got_ref[source, :, :].astype(F32)
    inverse = scale_ref[:, 0:1]
    rows = scale_ref[:, 1:2]
    unit = unit_ref[...]
    scaled = total[:, :width] * gain_ref[...]
    mean = jnp.sum(scaled * unit, axis=1, keepdims=True) * (1.0 / width)
    grad = cot_ref[...].astype(F32) + inverse * (scaled - unit * mean)
    times_cols = grad * cols_ref[...]
    grad_rows = jnp.sum(times_cols * base_ref[...], axis=1, keepdims=True)
    grad_base = times_cols * rows
    cols = total[:pieces, width:]
    spare = BLOCK - 2 * pieces
    line = jnp.sum(
        jnp.where(iota((BLOCK, LANES), 1) == iota((BLOCK, LANES), 0) + HALF, grad_rows, 0.0),
        axis=0,
        keepdims=True,
    )
    under = jnp.where(iota((spare, LANES), 0) == 0, line, 0.0)
    tail = jnp.concatenate([cols, swap_halves(cols), under], axis=0)
    first_half = iota((BLOCK, LANES), 1) < HALF
    for pair in range(width // LANES):
        block = grad_base[:, pair * LANES : (pair + 1) * LANES]
        out_ref[2 * pair, :, :] = jnp.where(first_half, block, tail).astype(BF16)
        out_ref[2 * pair + 1, :, :] = jnp.where(first_half, swap_halves(block), tail).astype(BF16)


def owner_kernel(first_ref, slot_ref, back_ref, shared_ref, col_ref):
    owned, width = col_ref.shape
    count = slot_ref.shape[1]
    pieces = width // LANES
    picker = (slot_ref[...] - first_ref[0] == iota((owned, count), 0)).astype(BF16)
    back = back_ref[...].astype(F32)
    total = jnp.sum(back, axis=0)
    first_half = iota((owned, LANES), 1) < HALF
    for piece in range(pieces):
        upper = dot(picker, back[:, piece, :].astype(BF16), 1, 0)
        lower = dot(picker, back[:, pieces + piece, :].astype(BF16), 1, 0)
        col_ref[:, piece * LANES : (piece + 1) * LANES] = jnp.where(
            first_half, swap_halves(lower), upper
        )
    rows = dot(back[:, 2 * pieces, :].astype(BF16), picker, 0, 1)
    shared = jnp.concatenate([total[:, :HALF], rows[HALF : HALF + BLOCK, :]], axis=1)
    shared_ref[...] = jnp.broadcast_to(shared[None], shared_ref.shape)


def update_kernel(grads_ref, *refs):
    grads = jnp.transpose(grads_ref[...])
    for kind in range(2):
        param, one, two, param_out, one_out, two_out = refs[kind::2]
        rows = param.shape[0]
        found = grads[kind * HALF : kind * HALF + rows, : param.shape[1]]
        param_out[...], one_out[...], two_out[...] = adam_step(param[...], one[...], two[...], found)


def local(
    hidden_rows,
    norm_gain,
    w_query,
    w_key,
    w_value,
    head_cotangent,
    prompt_cotangent,
    prompt_master,
    prompt_first,
    prompt_second,
    row_factor,
    row_first,
    row_second,
    col_factor,
    col_first,
    col_second,
    row_tenant,
    tenant_slot,
):
    dp, mp = ROWS_AXES, HEADS_AXES
    count = lax.axis_size(dp)
    groups = lax.axis_size(mp)
    device = lax.axis_index(dp)
    member = lax.axis_index(mp)
    owned, col_width = col_factor.shape
    width = hidden_rows.shape[2]
    pieces = col_width // LANES

    depth = w_query.shape[0]
    inner = w_query.shape[1]
    ring = lax.axis_size("y")
    pair = pl.pallas_call(
        lambda *refs: lead_kernel(owned, *refs),
        out_shape=jax.ShapeDtypeStruct((depth, 2 * inner + LANES), BF16),
        in_specs=[SMEM, SMEM, VMEM, VMEM],
        out_specs=VMEM,
        compiler_params=ALONE_PARAMS,
    )(row_tenant, tenant_slot, w_key, w_value)
    pair = lax.all_gather(pair, "y", axis=0, tiled=True)
    marks = pair.reshape(ring, depth, -1)[:, 0, 2 * inner : 2 * inner + 2].reshape(-1)
    pair = pair[:, : 2 * inner]

    marks = jnp.broadcast_to(
        jnp.pad(marks, (0, LANES - PROMPT - marks.shape[0]))[None], (depth, LANES - PROMPT)
    )
    own = jnp.concatenate([w_query, prompt_master.T.astype(BF16), marks], axis=1)
    pair, own = lax.optimization_barrier((pair, own))
    pair = lax.all_gather(pair, "z", axis=0, tiled=True)
    own = lax.all_gather(own, "z", axis=0, tiled=False)
    marks = own[:, 0, inner + PROMPT : inner + PROMPT + 2 * ring].reshape(count, 2)
    marks = marks.astype(jnp.int32)
    slots = (marks[:, 0] * owned + marks[:, 1])[None, :]
    first = (device * owned).astype(jnp.int32).reshape(1)
    terms = pl.pallas_call(
        factor_kernel,
        out_shape=jax.ShapeDtypeStruct((count, 8, LANES), F32),
        in_specs=[SMEM, VMEM, VMEM, VMEM],
        out_specs=VMEM,
        compiler_params=ALONE_PARAMS,
    )(first, slots, row_factor, col_factor)
    own, terms = lax.optimization_barrier((own, terms))
    terms = jnp.sum(lax.all_to_all(terms, dp, 0, 0, tiled=False), axis=0)
    half = own.shape[0] // 2
    up_ring = [(i, (i + 1) % ring) for i in range(ring)]
    down_ring = [(i, (i - 1) % ring) for i in range(ring)]
    left = lax.ppermute(own, "y", up_ring)
    right = lax.ppermute(own, "y", down_ring)
    far_first = lax.ppermute(left[:half], "y", up_ring)
    far_second = lax.ppermute(right[half:], "y", down_ring)
    singles = (own, left, right, far_first, far_second)
    factor_cols = lax.all_to_all(
        jnp.broadcast_to(terms[None], (groups, 8, LANES)), mp, 0, 0, tiled=False
    )
    factor_rows = terms[pieces : pieces + 1]

    gain = norm_gain[None, :]
    hidden = hidden_rows[0].astype(F32)
    inverse = lax.rsqrt(jnp.mean(hidden * hidden, axis=-1, keepdims=True) + norm_epsilon)
    hidden = (hidden * inverse * gain).astype(BF16)
    upstream = jnp.concatenate(
        [
            jnp.pad(head_cotangent[0, :PROMPT], ((0, PAD - PROMPT), (0, 0))),
            head_cotangent[0, PROMPT:],
        ],
        axis=0,
    )
    cot = lax.dynamic_slice_in_dim(
        jnp.pad(prompt_cotangent[0], ((0, PAD - PROMPT), (0, 0))), member * BLOCK, BLOCK, 0
    )
    y = lax.axis_index("y")
    place = jnp.stack(
        [member, lax.axis_index("c"), y, (y - 1) % ring, (y + 1) % ring, (y + 2) % ring]
    ).astype(jnp.int32)
    keep, send, unit_own, base_own, scale_own, line = main_part(
        place, pair, singles, hidden, upstream, factor_cols, factor_rows, gain, cot
    )

    other = lax.ppermute(send, "c", [(0, 1), (1, 0)])
    parts = (keep + other.astype(F32)).astype(BF16)
    parts = lax.all_to_all(parts, "x", 0, 0, tiled=False)
    outgoing = pl.pallas_call(
        lambda *refs: prompt_kernel(pieces, *refs),
        out_shape=jax.ShapeDtypeStruct((count, BLOCK, LANES), BF16),
        in_specs=[VMEM] * 7,
        out_specs=VMEM,
        compiler_params=PARAMS,
    )(parts, unit_own, base_own, cot, gain, line, scale_own)

    back = lax.all_to_all(outgoing, dp, 0, 0, tiled=False)
    shared, col_grad = pl.pallas_call(
        owner_kernel,
        out_shape=(
            jax.ShapeDtypeStruct((groups, BLOCK, LANES), F32),
            jax.ShapeDtypeStruct((owned, col_width), F32),
        ),
        in_specs=[SMEM, VMEM, VMEM],
        out_specs=(VMEM, VMEM),
        compiler_params=PARAMS,
    )(first, slots, back)
    shared = lax.all_to_all(shared, mp, 0, 0, tiled=False).reshape(PAD, LANES)
    operands = [
        part
        for pair in zip(
            (prompt_master.T, prompt_first.T, prompt_second.T), (row_factor, row_first, row_second)
        )
        for part in pair
    ]
    new = pl.pallas_call(
        update_kernel,
        out_shape=tuple(jax.ShapeDtypeStruct(part.shape, F32) for part in operands),
        in_specs=[VMEM] * 7,
        out_specs=(VMEM,) * 6,
        compiler_params=PARAMS,
    )(shared, *operands)
    return (
        *(part.T for part in new[0::2]),
        *new[1::2],
        *adam_step(col_factor, col_first, col_second, col_grad),
    )


def solution(mesh):
    ring = 4 if mesh.shape["dp"] % 4 == 0 else 2
    devices = mesh.devices.reshape(mesh.shape["dp"] // ring, ring, mesh.shape["mp"] // 2, 2)
    dp, mp = ROWS_AXES, HEADS_AXES
    return jax.shard_map(
        local,
        mesh=Mesh(devices, dp + mp),
        in_specs=(
            P(dp, None, None),
            P(),
            P(dp, mp),
            P(dp, mp),
            P(dp, mp),
            P(dp, None, mp),
            P(dp, None, None),
            P(None, dp),
            P(None, dp),
            P(None, dp),
            P(dp, None),
            P(dp, None),
            P(dp, None),
            P(dp, mp),
            P(dp, mp),
            P(dp, mp),
            P(dp),
            P(),
        ),
        out_specs=(
            P(None, dp),
            P(None, dp),
            P(None, dp),
            P(dp, None),
            P(dp, None),
            P(dp, None),
            P(dp, mp),
            P(dp, mp),
            P(dp, mp),
        ),
        check_vma=False,
    )
```
